512 devices in a mesh: kvp: 16 (over z, core), section: 4 (over x), tp: 8 (over y).
Axes of the slice: x: 4, y: 8, z: 8, core: 2. Of those that a mesh axis runs over, the one named last changes fastest.
Arguments:
- span: bfloat16 [4, 128, 8192], P('section', 'tp', 'kvp'), may hold values from -64 to 64
- gain: float32 [4, 8192], P('section', 'kvp'), may hold values from 0.1 to 1.9
- w_query: bfloat16 [4, 8192, 8192], P('section', 'kvp', 'tp'), may hold values from -0.0625 to 0.0625
- keys: bfloat16 [4, 65536, 8, 128], P('section', 'kvp', 'tp'), may hold values from -220 to 220
- values: bfloat16 [4, 65536, 8, 128], P('section', 'kvp', 'tp'), may hold values from -8 to 8
- lengths: int32 [16], P('kvp'), may hold values from 1 to 4096, as said below
- w_out: bfloat16 [4, 8192, 8192], P('section', 'tp', 'kvp'), may hold values from -0.0625 to 0.0625
Outputs:
- next_span: bfloat16 [4, 128, 8192], P('section', 'tp', 'kvp')
The draws below stay inside these ranges and needn't reach their ends.
Inputs may be any that keep to these rules, and one draw needn't show every extreme that they name: `lengths`: every shard but the last holds 4096 valid positions; the last holds 1 to 4096.
All inputs are finite; a program needn't handle non-finite values.
Results may differ from the reference program's by a relative error of at most 0.02.
Values may be sent and summed in bfloat16 or wider, within the bound.
No kernel may reach another device: no remote copies, remote signals or barrier semaphores. Data moves between devices by JAX's collectives and lax.ppermute only.
A program may use at most 64 MiB of HBM per device.

```python
import math
import jax
import jax.numpy as jnp
from jax import lax

D = 8192
HEADS = 64
KV_HEADS = 8
HD = 128
TQ = 128
KV_DEV = 4096
BLOCK = 512
SECTIONS = 4
KV_SHARDS = 16
CACHE = 65536


def draw_span(key, part):
    key = jax.random.fold_in(key, 11)
    first, second, third = jax.random.split(key, 3)
    column = jnp.arange(D, dtype=jnp.float32) / max(D - 1, 1)
    col_scale = jnp.exp(math.log(3.0) * column)[None, None, :] * jnp.exp(jax.random.uniform(second, (SECTIONS, 1, D), jnp.float32, -0.55, 0.55))
    base = jnp.clip(jax.random.normal(first, (SECTIONS, TQ, D), jnp.float32), -4.0, 4.0)
    row_scale = jnp.exp(jax.random.uniform(third, (SECTIONS, TQ, 1), jnp.float32, math.log(0.3), math.log(3.0)))
    return (0.3 * base * col_scale * row_scale).astype(jnp.bfloat16)


def draw_keys(key, part):
    key = jax.random.fold_in(key, 12)
    first = jax.random.fold_in(key, 0)
    shape = (SECTIONS, CACHE, KV_HEADS, HD)
    out = 3.0 * jnp.clip(jax.random.normal(first, shape, jnp.float32), -5.0, 5.0)
    return out.astype(jnp.bfloat16)


def draw_values(key, part):
    key = jax.random.fold_in(key, 13)
    first, second, third = jax.random.split(key, 3)
    shape = (SECTIONS, CACHE, KV_HEADS, HD)
    position = (jnp.arange(CACHE, dtype=jnp.float32) / CACHE)[None, :, None, None]
    freq = jax.random.uniform(second, (SECTIONS, 1, KV_HEADS, HD), jnp.float32, 0.3, 1.2)
    phase = jax.random.uniform(third, (SECTIONS, 1, KV_HEADS, HD), jnp.float32, -math.pi, math.pi)
    noise = jnp.clip(jax.random.normal(first, shape, jnp.float32), -4.0, 4.0)
    amplitude = 2.5
    smooth = amplitude * jnp.sin(2.0 * math.pi * freq * position + phase)
    return (noise + smooth).astype(jnp.bfloat16)


def draw_lengths(key, part):
    key = jax.random.fold_in(key, 14)
    whole = jax.random.randint(key, (), (KV_SHARDS - 1) * KV_DEV + 1, KV_SHARDS * KV_DEV + 1)
    starts = jnp.arange(KV_SHARDS, dtype=jnp.int32) * KV_DEV
    return jnp.clip(whole - starts, 0, KV_DEV).astype(jnp.int32)


def steps_of(stream_key, dims, pieces, least, largest):
    level, own = 1.0, jax.random.fold_in(stream_key, 6)
    for dim, parts in pieces:
        draws = jnp.exp(jax.random.uniform(jax.random.fold_in(own, dim), (parts,), jnp.float32, least / len(pieces), largest / len(pieces)))
        level = level * jnp.repeat(draws, dims[dim] // parts).reshape([-1 if axis == dim else 1 for axis in range(len(dims))])
    return level


def scatter_about(rng, dims, scale, bound, cuts=(), kind=jnp.bfloat16):
    loudness = steps_of(rng, dims, cuts, -0.22, 0.18) if cuts else 1.0
    values = jax.random.normal(rng, dims, jnp.float32) * scale * loudness
    return jnp.minimum(jnp.maximum(values, -bound), bound).astype(kind)


def setup_inputs(seed: int = 0) -> dict:
    streams_of = jax.random.split(jax.random.key(seed), 8)
    span = draw_span(jax.random.fold_in(streams_of[7], 71), 0)
    gain = jnp.clip(1.0 + 0.18 * jax.random.normal(streams_of[1], (SECTIONS, D), jnp.float32), 0.1, 1.9)
    w_query = scatter_about(streams_of[2], (SECTIONS, D, HEADS * HD), D ** -0.5, 0.0625, ((0, 4), (1, 16), (2, 8)))
    keys = draw_keys(jax.random.fold_in(streams_of[7], 71), 0)
    values = draw_values(jax.random.fold_in(streams_of[7], 71), 0)
    lengths = draw_lengths(jax.random.fold_in(streams_of[7], 71), 0)
    w_out = scatter_about(streams_of[6], (SECTIONS, HEADS * HD, D), (HEADS * HD) ** -0.5, 0.0625, ((0, 4), (1, 8), (2, 16)))
    return {"span": span, "gain": gain, "w_query": w_query, "keys": keys, "values": values, "lengths": lengths, "w_out": w_out}


EPS = 1e-05
NEG = -1e+30

def combine_pair(first, second):
    best = jnp.maximum(first[0], second[0])
    left = jnp.exp(first[0] - best)
    right = jnp.exp(second[0] - best)
    total = first[1] * left + second[1] * right
    accum = first[2] * left[..., None] + second[2] * right[..., None]
    return (best, total, accum)

def block_partials(query_heads, key_block, value_block, valid_mask):
    scores = jnp.einsum('tghd,jgd->ghtj', query_heads, key_block.astype(jnp.float32)) * (1.0 / math.sqrt(HD))
    scores = jnp.where(valid_mask, scores, NEG)
    top = lax.optimization_barrier(jnp.max(scores, axis=3))
    probs = jnp.where(valid_mask, jnp.exp(scores - top[..., None]), 0.0).astype(jnp.bfloat16)
    total = lax.optimization_barrier(jnp.sum(probs.astype(jnp.float32), axis=3))
    accum = jnp.einsum('ghtj,jgd->ghtd', probs.astype(jnp.float32), value_block.astype(jnp.float32))
    return (top, total, accum)

def shard_partials(query_heads, shard_keys, shard_values, length):
    blocks = KV_DEV // BLOCK
    key_blocks = shard_keys.reshape(blocks, BLOCK, KV_HEADS, HD)
    value_blocks = shard_values.reshape(blocks, BLOCK, KV_HEADS, HD)
    position = jnp.arange(KV_DEV, dtype=jnp.int32).reshape(blocks, BLOCK)
    group = HEADS // KV_HEADS
    start = (jnp.full((KV_HEADS, group, TQ), NEG, jnp.float32), jnp.zeros((KV_HEADS, group, TQ), jnp.float32), jnp.zeros((KV_HEADS, group, TQ, HD), jnp.float32))

    def step(carry, item):
        piece = block_partials(query_heads, item[0], item[1], item[2] < length)
        return (combine_pair(carry, piece), None)
    result, unused = lax.scan(step, start, (key_blocks, value_blocks, position))
    return result

def reference(span, gain, w_query, keys, values, lengths, w_out):
    group = HEADS // KV_HEADS
    results = []
    for section in range(SECTIONS):
        wide = span[section].astype(jnp.float32)
        square = lax.optimization_barrier(jnp.sum(wide * wide, axis=1))
        normed = (wide * lax.rsqrt(square / D + EPS)[:, None] * gain[section][None, :]).astype(jnp.bfloat16)
        query = jnp.dot(normed, w_query[section], preferred_element_type=jnp.float32).astype(jnp.bfloat16)
        query_heads = query.reshape(TQ, KV_HEADS, group, HD).astype(jnp.float32)
        shard_keys = keys[section].reshape(KV_SHARDS, KV_DEV, KV_HEADS, HD)
        shard_values = values[section].reshape(KV_SHARDS, KV_DEV, KV_HEADS, HD)
        tops, totals, accums = lax.map(lambda item: shard_partials(query_heads, item[0], item[1], item[2]), (shard_keys, shard_values, lengths))
        best = lax.optimization_barrier(jnp.max(tops, axis=0))
        factor = jnp.exp(tops - best[None])
        denom = lax.optimization_barrier(jnp.sum(totals * factor, axis=0))
        numer = lax.optimization_barrier(jnp.sum(accums * factor[..., None], axis=0))
        attended = (numer / denom[..., None]).astype(jnp.bfloat16)
        attended = jnp.transpose(attended, (2, 0, 1, 3)).reshape(TQ, HEADS * HD)
        projected = jnp.dot(attended, w_out[section], preferred_element_type=jnp.float32)
        results.append((projected + wide).astype(jnp.bfloat16))
    stacked = jnp.stack(results, axis=0)
    return jnp.roll(stacked, 1, axis=0)
```

```python
import functools
import math

import jax
import jax.numpy as jnp
from jax import lax
from jax.experimental import pallas as pl
from jax.experimental.pallas import tpu as pltpu
from jax.sharding import Mesh, PartitionSpec as P

D = 8192
HEADS = 64
KV_HEADS = 8
HD = 128
EPS = 1e-05

GROUP = HEADS // KV_HEADS
CORES = 2
OWN = GROUP // CORES
LANES = 128
STAT_ROWS = 8
ONES_ROWS = 16
VALUE_ROWS = HD + ONES_ROWS
PIECE = 1024

QUERY_SCALE = 128.0
ACCUM_SCALE = 4096.0
OUT_SCALE = 64.0
LEVEL_STEP = 256.0

def from_behind(value, axis, steps):
    count = lax.axis_size(axis)
    pairs = [(source, (source + steps) % count) for source in range(count)]
    return lax.ppermute(value, axis, pairs)


def spread(value, axis):
    count = lax.psum(1, axis)
    return lax.all_to_all(jnp.broadcast_to(value[None], (count,) + value.shape), axis, 0, 0)


def square_kernel(span, out):
    wide = span[...].astype(jnp.float32)
    square = jnp.sum(wide * wide, axis=1, keepdims=True)
    step = wide.shape[0]
    at = lax.broadcasted_iota(jnp.int32, (step, LANES), 0)
    lane = lax.broadcasted_iota(jnp.int32, (step, LANES), 1)
    row = jnp.sum(jnp.where(at == lane, square, 0.0), axis=0, keepdims=True)
    out[...] = jnp.broadcast_to(row[None], out.shape)


def norm_kernel(squares, span, gain, out):
    wide = span[...].astype(jnp.float32)
    step = wide.shape[0]
    row = jnp.sum(squares[...], axis=0)
    at = lax.broadcasted_iota(jnp.int32, (step, LANES), 0)
    lane = lax.broadcasted_iota(jnp.int32, (step, LANES), 1)
    square = jnp.sum(jnp.where(at == lane, row, 0.0), axis=1, keepdims=True)
    normed = (wide * lax.rsqrt(square / D + EPS) * gain[...]).astype(jnp.bfloat16)
    out[...] = jnp.broadcast_to(normed[None], out.shape)


def project_kernel(normed, weight, out, *, chips):
    width = weight.shape[1] // CORES
    step = normed.shape[0] // chips
    for core in range(CORES):
        part = jnp.dot(
            normed[...],
            weight[:, core * width : (core + 1) * width],
            preferred_element_type=jnp.float32,
        )
        out[core * chips : (core + 1) * chips] = part.reshape(chips, step, width) * QUERY_SCALE


def small_call(kernel, shape, dtype, *operands):
    return pl.pallas_call(
        kernel,
        out_shape=jax.ShapeDtypeStruct(shape, dtype),
        in_specs=[pl.BlockSpec(memory_space=pltpu.VMEM)] * len(operands),
        out_specs=pl.BlockSpec(memory_space=pltpu.VMEM),
        compiler_params=pltpu.CompilerParams(vmem_limit_bytes=8 * 1024 * 1024),
    )(*operands)


def key_row(position):
    step, at = divmod(position, PIECE)
    return step * (PIECE + VALUE_ROWS * (PIECE // LANES)) + at


def value_row(position):
    step, at = divmod(position, PIECE)
    return key_row(step * PIECE) + PIECE + at // LANES * VALUE_ROWS


def prepare_kernel(length, keys, values, after, out):
    del after
    count = keys.shape[0]
    valid = length[0]
    at = lax.broadcasted_iota(jnp.int32, (HD, HD), 0)
    lane = lax.broadcasted_iota(jnp.int32, (HD, HD), 1)
    unit = jnp.where(at == lane, 1.0, 0.0).astype(jnp.bfloat16)

    def write(masked):
        for start in range(0, count, PIECE):
            own_keys = keys[start : start + PIECE, :]
            own_values = values[start : start + PIECE, :]
            if masked:
                inside = start + lax.broadcasted_iota(jnp.int32, (PIECE, HD), 0) < valid
                first = keys[0:16, :].astype(jnp.float32)[0:1, :]
                own_keys = jnp.where(inside, own_keys.astype(jnp.float32), first)
                own_keys = own_keys.astype(jnp.bfloat16)
                own_values = jnp.where(inside, own_values.astype(jnp.float32), 0.0)
                own_values = own_values.astype(jnp.bfloat16)
            out[key_row(start) : key_row(start) + PIECE, :] = own_keys
            across = lax.dot_general(
                unit, own_values, (((1,), (1,)), ((), ())), preferred_element_type=jnp.float32
            ).astype(jnp.bfloat16)
            for block in range(0, PIECE, LANES):
                row = value_row(start + block)
                out[row : row + HD, :] = across[:, block : block + LANES]
                ones = jnp.ones((ONES_ROWS, LANES), jnp.float32)
                if masked:
                    place = lax.broadcasted_iota(jnp.int32, (ONES_ROWS, LANES), 1)
                    ones = jnp.where(start + block + place < valid, ones, 0.0)
                out[row + HD : row + VALUE_ROWS, :] = ones.astype(jnp.bfloat16)

    pl.when(valid >= count)(functools.partial(write, False))
    pl.when(valid < count)(functools.partial(write, True))


def prepare(lengths, keys, values, after):
    count = keys.shape[0]
    return pl.pallas_call(
        prepare_kernel,
        out_shape=jax.ShapeDtypeStruct((key_row(count), HD), jnp.bfloat16),
        in_specs=[
            pl.BlockSpec(memory_space=pltpu.SMEM),
            pl.BlockSpec(memory_space=pltpu.VMEM),
            pl.BlockSpec(memory_space=pltpu.VMEM),
            pl.BlockSpec(memory_space=pl.ANY),
        ],
        out_specs=pl.BlockSpec(memory_space=pltpu.VMEM),
        compiler_params=pltpu.CompilerParams(vmem_limit_bytes=16 * 1024 * 1024),
        cost_estimate=pl.CostEstimate(
            flops=8 * count * HD, bytes_accessed=8 * count * HD, transcendentals=0
        ),
    )(lengths, keys, values, after)


def attend_kernel(query, here, there, out, scores, *, chunks):
    tokens = query.shape[0]
    wide = 2 * tokens
    cache = (here, there)
    count = scores.shape[1]
    pieces = count // PIECE
    pairs = OWN // 2
    unit = math.log2(math.e) / math.sqrt(HD)

    def query_pair(pair):
        base = pair * 2 * HD
        return jnp.concatenate(
            [query[:, base : base + HD], query[:, base + HD : base + 2 * HD]], axis=0
        )

    def score_piece(number, pair_query, piece, top):
        half, pair = divmod(number, pairs)
        part = lax.dot_general(
            cache[half][key_row(piece * PIECE) : key_row(piece * PIECE) + PIECE, :],
            pair_query,
            (((1,), (1,)), ((), ())),
            preferred_element_type=jnp.float32,
        )
        scores[number % 2, piece * PIECE : (piece + 1) * PIECE, :] = part
        return jnp.maximum(top, jnp.max(part.reshape(PIECE // 8, 8, wide), axis=0))

    first = jnp.full((8, wide), -jnp.inf, jnp.float32)
    top = first
    ahead = query_pair(0)
    for piece in range(pieces):
        top = score_piece(0, ahead, piece, top)
    held = []
    for number in range(CORES * pairs):
        half, pair = divmod(number, pairs)
        best = jnp.max(top, axis=0, keepdims=True)
        top = first
        more = number + 1 < CORES * pairs
        if more:
            ahead = query_pair((number + 1) % pairs)
        accum = jnp.zeros((VALUE_ROWS, wide), jnp.float32)
        for piece in range(pieces):
            if more:
                top = score_piece(number + 1, ahead, piece, top)
            span = slice(piece * PIECE, (piece + 1) * PIECE)
            weight = jnp.exp2((scores[number % 2, span, :] - best) * unit).astype(jnp.bfloat16)
            across = [
                cache[half][value_row(start) : value_row(start) + VALUE_ROWS, :]
                for start in range(piece * PIECE, (piece + 1) * PIECE, LANES)
            ]
            accum += jnp.dot(
                jnp.concatenate(across, axis=1), weight, preferred_element_type=jnp.float32
            )
        held.append((best, accum))
        if half + 1 < CORES:
            continue

        best_here, accum_here = held[pair]
        both = jnp.maximum(best_here, best)
        accum = accum_here * jnp.exp2((best_here - both) * unit) + accum * jnp.exp2(
            (best - both) * unit
        )
        total = accum[HD : HD + 1, :]
        level = both * unit + jnp.log2(total)
        high = jnp.where(jnp.abs(level) < 1.0, 0.0, level).astype(jnp.bfloat16).astype(jnp.float32)
        rest = level - high
        middle = rest.astype(jnp.bfloat16).astype(jnp.float32)
        stats = jnp.concatenate(
            [
                high * (1.0 / LEVEL_STEP),
                middle,
                (rest - middle) * LEVEL_STEP,
                jnp.zeros((STAT_ROWS - 3, wide), jnp.float32),
            ],
            axis=0,
        )
        mean = accum[0:HD, :] * (ACCUM_SCALE / total)
        per_head = chunks // OWN
        rows = HD // per_head
        for side in range(2):
            lanes = slice(side * tokens, (side + 1) * tokens)
            for part in range(per_head):
                chunk = (2 * pair + side) * per_head + part
                out[chunk, 0:rows, :] = mean[part * rows : (part + 1) * rows, lanes]
                out[chunk, rows : rows + STAT_ROWS, :] = stats[:, lanes]


def attend(query, here, there, count, chunks):
    tokens = query.shape[0]
    rows = OWN * HD // chunks
    return pl.pallas_call(
        functools.partial(attend_kernel, chunks=chunks),
        out_shape=jax.ShapeDtypeStruct((chunks, rows + STAT_ROWS, tokens), jnp.float32),
        in_specs=[pl.BlockSpec(memory_space=pltpu.VMEM)] * 3,
        out_specs=pl.BlockSpec(memory_space=pltpu.VMEM),
        scratch_shapes=[pltpu.VMEM((2, count, 2 * tokens), jnp.float32)],
        compiler_params=pltpu.CompilerParams(vmem_limit_bytes=24 * 1024 * 1024),
        cost_estimate=pl.CostEstimate(
            flops=4 * GROUP * tokens * count * HD,
            bytes_accessed=8 * count * HD,
            transcendentals=GROUP * tokens * count,
        ),
    )(query, here, there)


def local(span, gain, w_query, keys, values, lengths, w_out):
    chips = lax.axis_size("z")
    shards = CORES * chips
    heads = lax.axis_size("tp")
    own = span[0]
    step = own.shape[0]
    tokens = heads * step
    width = GROUP * HD

    squares = small_call(square_kernel, (shards, 1, LANES), jnp.float32, own)
    here = prepare(lengths, keys[0, :, 0, :], values[0, :, 0, :], squares)
    squares = lax.all_to_all(squares, ("core", "z"), 0, 0)
    squares, here = lax.optimization_barrier((squares, here))
    there = from_behind(here, "core", 1)
    normed = small_call(norm_kernel, (heads,) + own.shape, jnp.bfloat16, squares, own, gain)
    normed = lax.all_to_all(normed, "tp", 0, 0).reshape(tokens, -1)

    partial = small_call(
        functools.partial(project_kernel, chips=chips),
        (shards, tokens // chips, width // CORES),
        jnp.float32,
        normed,
        w_query[0],
    )
    parts = lax.all_to_all(partial.astype(jnp.float16), ("core", "z"), 0, 0)
    query = jnp.sum(parts.astype(jnp.float32), axis=0) * (1.0 / QUERY_SCALE)
    query = spread(query.astype(jnp.bfloat16), "z").reshape(tokens, width // CORES)

    rows = width // shards
    pieces = attend(query, here, there, keys.shape[1], chips).astype(jnp.float16)
    pieces = lax.all_to_all(pieces, "z", 0, 0).astype(jnp.float32)
    level = (
        pieces[:, rows, :] * LEVEL_STEP
        + pieces[:, rows + 1, :]
        + pieces[:, rows + 2, :] * (1.0 / LEVEL_STEP)
    )
    factor = jnp.exp2(level - jnp.max(level, axis=0, keepdims=True))
    numer = jnp.sum(pieces[:, :rows, :] * factor[:, None, :], axis=0)
    denom = jnp.sum(factor, axis=0, keepdims=True) * ACCUM_SCALE
    attended = spread((numer / denom).astype(jnp.bfloat16), ("core", "z")).reshape(width, tokens)

    projected = lax.dot_general(
        attended, w_out[0], (((0,), (0,)), ((), ())), preferred_element_type=jnp.float32
    )
    projected = (projected * OUT_SCALE).astype(jnp.float16).reshape(heads, step, -1)
    parts = lax.all_to_all(projected, "tp", 0, 0).astype(jnp.float32)
    updated = (own.astype(jnp.float32) + jnp.sum(parts, axis=0) * (1.0 / OUT_SCALE)).astype(jnp.bfloat16)
    return from_behind(updated, "section", 1)[None]


def solution(mesh):
    shards, sections, heads = (mesh.shape[name] for name in ("kvp", "section", "tp"))
    split = Mesh(
        mesh.devices.reshape(shards // CORES, CORES, sections, heads),
        ("z", "core", "section", "tp"),
    )
    shard = ("z", "core")
    in_specs = (
        P("section", "tp", shard),
        P("section", shard),
        P("section", shard, "tp"),
        P("section", shard, "tp", None),
        P("section", shard, "tp", None),
        P(shard),
        P("section", "tp", shard),
    )
    out_specs = P("section", "tp", shard)
    return jax.shard_map(local, mesh=split, in_specs=in_specs, out_specs=out_specs, check_vma=False)
```

```python
import functools
import math

import jax
import jax.numpy as jnp
from jax import lax
from jax.experimental import pallas as pl
from jax.experimental.pallas import tpu as pltpu
from jax.sharding import Mesh, PartitionSpec as P

D = 8192
HEADS = 64
KV_HEADS = 8
HD = 128
EPS = 1e-05

GROUP = HEADS // KV_HEADS
CORES = 2
OWN = GROUP // CORES
LANES = 128
STAT_ROWS = 8
ONES_ROWS = 16
VALUE_ROWS = HD + ONES_ROWS
PIECE = 512
REACH = 2048

QUERY_SCALE = 128.0
ACCUM_SCALE = 4096.0
OUT_SCALE = 64.0
LEVEL_STEP = 256.0

def from_behind(value, axis, steps):
    count = lax.axis_size(axis)
    pairs = [(source, (source + steps) % count) for source in range(count)]
    return lax.ppermute(value, axis, pairs)


def spread(value, axis):
    count = lax.psum(1, axis)
    return lax.all_to_all(jnp.broadcast_to(value[None], (count,) + value.shape), axis, 0, 0)


def square_kernel(span, out):
    wide = span[...].astype(jnp.float32)
    square = jnp.sum(wide * wide, axis=1, keepdims=True)
    step = wide.shape[0]
    at = lax.broadcasted_iota(jnp.int32, (step, LANES), 0)
    lane = lax.broadcasted_iota(jnp.int32, (step, LANES), 1)
    row = jnp.sum(jnp.where(at == lane, square, 0.0), axis=0, keepdims=True)
    out[...] = jnp.broadcast_to(row[None], out.shape)


def norm_kernel(squares, span, gain, out):
    wide = span[...].astype(jnp.float32)
    step = wide.shape[0]
    row = jnp.sum(squares[...], axis=0)
    at = lax.broadcasted_iota(jnp.int32, (step, LANES), 0)
    lane = lax.broadcasted_iota(jnp.int32, (step, LANES), 1)
    square = jnp.sum(jnp.where(at == lane, row, 0.0), axis=1, keepdims=True)
    normed = (wide * lax.rsqrt(square / D + EPS) * gain[...]).astype(jnp.bfloat16)
    out[...] = jnp.broadcast_to(normed[None], out.shape)


def small_call(kernel, shape, dtype, *operands):
    return pl.pallas_call(
        kernel,
        out_shape=jax.ShapeDtypeStruct(shape, dtype),
        in_specs=[pl.BlockSpec(memory_space=pltpu.VMEM)] * len(operands),
        out_specs=pl.BlockSpec(memory_space=pltpu.VMEM),
        compiler_params=pltpu.CompilerParams(vmem_limit_bytes=8 * 1024 * 1024),
    )(*operands)


def key_row(position):
    step, at = divmod(position, PIECE)
    return step * (PIECE + VALUE_ROWS * (PIECE // LANES)) + at


def value_row(position):
    step, at = divmod(position, PIECE)
    return key_row(step * PIECE) + PIECE + at // LANES * VALUE_ROWS


def prepare_kernel(length, keys, values, after, out):
    del after
    count = keys.shape[0]
    valid = length[0]
    at = lax.broadcasted_iota(jnp.int32, (HD, HD), 0)
    lane = lax.broadcasted_iota(jnp.int32, (HD, HD), 1)
    unit = jnp.where(at == lane, 1.0, 0.0).astype(jnp.bfloat16)

    def write(masked):
        for start in range(0, count, PIECE):
            own_keys = keys[start : start + PIECE, :]
            own_values = values[start : start + PIECE, :]
            if masked:
                inside = start + lax.broadcasted_iota(jnp.int32, (PIECE, HD), 0) < valid
                first = keys[0:16, :].astype(jnp.float32)[0:1, :]
                own_keys = jnp.where(inside, own_keys.astype(jnp.float32), first)
                own_keys = own_keys.astype(jnp.bfloat16)
                own_values = jnp.where(inside, own_values.astype(jnp.float32), 0.0)
                own_values = own_values.astype(jnp.bfloat16)
            out[key_row(start) : key_row(start) + PIECE, :] = own_keys
            across = lax.dot_general(
                unit, own_values, (((1,), (1,)), ((), ())), preferred_element_type=jnp.float32
            ).astype(jnp.bfloat16)
            for block in range(0, PIECE, LANES):
                row = value_row(start + block)
                out[row : row + HD, :] = across[:, block : block + LANES]
                ones = jnp.ones((ONES_ROWS, LANES), jnp.float32)
                if masked:
                    place = lax.broadcasted_iota(jnp.int32, (ONES_ROWS, LANES), 1)
                    ones = jnp.where(start + block + place < valid, ones, 0.0)
                out[row + HD : row + VALUE_ROWS, :] = ones.astype(jnp.bfloat16)

    pl.when(valid >= count)(functools.partial(write, False))
    pl.when(valid < count)(functools.partial(write, True))


def prepare(lengths, keys, values, after):
    count = keys.shape[0]
    return pl.pallas_call(
        prepare_kernel,
        out_shape=jax.ShapeDtypeStruct((key_row(count), HD), jnp.bfloat16),
        in_specs=[
            pl.BlockSpec(memory_space=pltpu.SMEM),
            pl.BlockSpec(memory_space=pltpu.VMEM),
            pl.BlockSpec(memory_space=pltpu.VMEM),
            pl.BlockSpec(memory_space=pl.ANY),
        ],
        out_specs=pl.BlockSpec(memory_space=pltpu.VMEM),
        compiler_params=pltpu.CompilerParams(vmem_limit_bytes=16 * 1024 * 1024),
        cost_estimate=pl.CostEstimate(
            flops=8 * count * HD, bytes_accessed=8 * count * HD, transcendentals=0
        ),
    )(lengths, keys, values, after)


def attend_kernel(query, here, there, out, scores, *, chunks, count):
    tokens = query.shape[0]
    wide = 2 * tokens
    cache = (here, there)
    reach = scores.shape[1]
    pairs = OWN // 2
    unit = math.log2(math.e) / math.sqrt(HD)
    units = [
        (half, start, pair)
        for half in range(CORES)
        for start in range(0, count, reach)
        for pair in range(pairs)
    ]

    def query_pair(pair):
        base = pair * 2 * HD
        return jnp.concatenate(
            [query[:, base : base + HD], query[:, base + HD : base + 2 * HD]], axis=0
        )

    queries = [query_pair(pair) for pair in range(pairs)]

    def score_piece(number, offset, top):
        half, start, pair = units[number]
        row = key_row(start + offset)
        part = lax.dot_general(
            cache[half][row : row + PIECE, :],
            queries[pair],
            (((1,), (1,)), ((), ())),
            preferred_element_type=jnp.float32,
        )
        scores[number % 2, offset : offset + PIECE, :] = part
        return jnp.maximum(top, jnp.max(part.reshape(PIECE // 8, 8, wide), axis=0))

    lowest = jnp.full((8, wide), -jnp.inf, jnp.float32)
    top = lowest
    for offset in range(0, reach, PIECE):
        top = score_piece(0, offset, top)
    held = [None] * pairs
    for number, (half, start, pair) in enumerate(units):
        best = jnp.max(top, axis=0, keepdims=True)
        top = lowest
        accum = jnp.zeros((VALUE_ROWS, wide), jnp.float32)
        for offset in range(0, reach, PIECE):
            if number + 1 < len(units):
                top = score_piece(number + 1, offset, top)
            weight = jnp.exp2((scores[number % 2, offset : offset + PIECE, :] - best) * unit)
            across = [
                cache[half][value_row(at) : value_row(at) + VALUE_ROWS, :]
                for at in range(start + offset, start + offset + PIECE, LANES)
            ]
            accum += jnp.dot(
                jnp.concatenate(across, axis=1),
                weight.astype(jnp.bfloat16),
                preferred_element_type=jnp.float32,
            )
        if held[pair] is not None:
            before, summed = held[pair]
            both = jnp.maximum(before, best)
            accum = summed * jnp.exp2((before - both) * unit) + accum * jnp.exp2(
                (best - both) * unit
            )
            best = both
        held[pair] = (best, accum)

    for pair in range(pairs):
        best, accum = held[pair]
        total = accum[HD : HD + 1, :]
        level = best * unit + jnp.log2(total)
        high = jnp.where(jnp.abs(level) < 1.0, 0.0, level).astype(jnp.bfloat16).astype(jnp.float32)
        rest = level - high
        middle = rest.astype(jnp.bfloat16).astype(jnp.float32)
        stats = jnp.concatenate(
            [
                high * (1.0 / LEVEL_STEP),
                middle,
                (rest - middle) * LEVEL_STEP,
                jnp.zeros((STAT_ROWS - 3, wide), jnp.float32),
            ],
            axis=0,
        )
        mean = accum[0:HD, :] * (ACCUM_SCALE / total)
        per_head = chunks // OWN
        rows = HD // per_head
        for side in range(2):
            lanes = slice(side * tokens, (side + 1) * tokens)
            for part in range(per_head):
                chunk = (2 * pair + side) * per_head + part
                out[chunk, 0:rows, :] = mean[part * rows : (part + 1) * rows, lanes]
                out[chunk, rows : rows + STAT_ROWS, :] = stats[:, lanes]


def attend(query, here, there, count, chunks):
    tokens = query.shape[0]
    rows = OWN * HD // chunks
    return pl.pallas_call(
        functools.partial(attend_kernel, chunks=chunks, count=count),
        out_shape=jax.ShapeDtypeStruct((chunks, rows + STAT_ROWS, tokens), jnp.float32),
        in_specs=[pl.BlockSpec(memory_space=pltpu.VMEM)] * 3,
        out_specs=pl.BlockSpec(memory_space=pltpu.VMEM),
        scratch_shapes=[pltpu.VMEM((2, min(count, REACH), 2 * tokens), jnp.float32)],
        compiler_params=pltpu.CompilerParams(vmem_limit_bytes=24 * 1024 * 1024),
        cost_estimate=pl.CostEstimate(
            flops=4 * GROUP * tokens * count * HD,
            bytes_accessed=8 * count * HD,
            transcendentals=GROUP * tokens * count,
        ),
    )(query, here, there)


def local(span, gain, w_query, keys, values, lengths, w_out):
    chips = lax.axis_size("z")
    shards = CORES * chips
    heads = lax.axis_size("tp")
    own = span[0]
    step = own.shape[0]
    tokens = heads * step
    width = GROUP * HD

    squares = small_call(square_kernel, (shards, 1, LANES), jnp.float32, own)
    here = prepare(lengths, keys[0, :, 0, :], values[0, :, 0, :], squares)
    squares = lax.all_to_all(squares, ("core", "z"), 0, 0)
    squares, here = lax.optimization_barrier((squares, here))
    there = from_behind(here, "core", 1)
    normed = small_call(norm_kernel, (heads,) + own.shape, jnp.bfloat16, squares, own, gain)
    normed = lax.all_to_all(normed, "tp", 0, 0).reshape(tokens, -1)

    partial = jnp.dot(normed, w_query[0], preferred_element_type=jnp.float32) * QUERY_SCALE
    partial = partial.astype(jnp.float16).reshape(tokens, CORES, width // CORES)
    partial = jnp.swapaxes(partial, 0, 1).reshape(shards, tokens // chips, width // CORES)
    parts = lax.all_to_all(partial, ("core", "z"), 0, 0)
    query = jnp.sum(parts.astype(jnp.float32), axis=0) * (1.0 / QUERY_SCALE)
    query = spread(query.astype(jnp.bfloat16), "z").reshape(tokens, width // CORES)

    rows = width // shards
    pieces = attend(query, here, there, keys.shape[1], chips).astype(jnp.float16)
    pieces = lax.all_to_all(pieces, "z", 0, 0).astype(jnp.float32)
    level = (
        pieces[:, rows, :] * LEVEL_STEP
        + pieces[:, rows + 1, :]
        + pieces[:, rows + 2, :] * (1.0 / LEVEL_STEP)
    )
    factor = jnp.exp2(level - jnp.max(level, axis=0, keepdims=True))
    numer = jnp.sum(pieces[:, :rows, :] * factor[:, None, :], axis=0)
    denom = jnp.sum(factor, axis=0, keepdims=True) * ACCUM_SCALE
    attended = spread((numer / denom).astype(jnp.bfloat16), ("core", "z")).reshape(width, tokens)

    projected = lax.dot_general(
        attended, w_out[0], (((0,), (0,)), ((), ())), preferred_element_type=jnp.float32
    )
    projected = (projected * OUT_SCALE).astype(jnp.float16).reshape(heads, step, -1)
    parts = lax.all_to_all(projected, "tp", 0, 0).astype(jnp.float32)
    updated = (own.astype(jnp.float32) + jnp.sum(parts, axis=0) * (1.0 / OUT_SCALE)).astype(jnp.bfloat16)
    return from_behind(updated, "section", 1)[None]


def solution(mesh):
    shards, sections, heads = (mesh.shape[name] for name in ("kvp", "section", "tp"))
    split = Mesh(
        mesh.devices.reshape(shards // CORES, CORES, sections, heads),
        ("z", "core", "section", "tp"),
    )
    shard = ("z", "core")
    in_specs = (
        P("section", "tp", shard),
        P("section", shard),
        P("section", shard, "tp"),
        P("section", shard, "tp", None),
        P("section", shard, "tp", None),
        P(shard),
        P("section", "tp", shard),
    )
    out_specs = P("section", "tp", shard)
    return jax.shard_map(local, mesh=split, in_specs=in_specs, out_specs=out_specs, check_vma=False)
```

```python
import functools
import math

import jax
import jax.numpy as jnp
from jax import lax
from jax.experimental import pallas as pl
from jax.experimental.pallas import tpu as pltpu
from jax.sharding import Mesh, PartitionSpec as P

D = 8192
HEADS = 64
KV_HEADS = 8
HD = 128
EPS = 1e-05

GROUP = HEADS // KV_HEADS
CORES = 2
OWN = GROUP // CORES
LANES = 128
STAT_ROWS = 8
ONES_ROWS = 16
VALUE_ROWS = HD + ONES_ROWS
PIECE = 512
REACH = 1024

QUERY_SCALE = 128.0
ACCUM_SCALE = 4096.0
OUT_SCALE = 64.0
LEVEL_STEP = 256.0

def from_behind(value, axis, steps):
    count = lax.axis_size(axis)
    pairs = [(source, (source + steps) % count) for source in range(count)]
    return lax.ppermute(value, axis, pairs)


def spread(value, axis):
    count = lax.psum(1, axis)
    return lax.all_to_all(jnp.broadcast_to(value[None], (count,) + value.shape), axis, 0, 0)


def square_kernel(rows, out):
    wide = rows[...].astype(jnp.float32)
    square = jnp.sum(wide * wide, axis=1, keepdims=True)
    tokens = wide.shape[0]
    at = lax.broadcasted_iota(jnp.int32, (tokens, tokens), 0)
    lane = lax.broadcasted_iota(jnp.int32, (tokens, tokens), 1)
    row = jnp.sum(jnp.where(at == lane, square, 0.0), axis=0, keepdims=True)
    out[...] = jnp.broadcast_to(row[None], out.shape)


def norm_kernel(squares, rows, gain, out):
    wide = rows[...].astype(jnp.float32)
    tokens = wide.shape[0]
    row = jnp.sum(squares[...], axis=0)
    at = lax.broadcasted_iota(jnp.int32, (tokens, tokens), 0)
    lane = lax.broadcasted_iota(jnp.int32, (tokens, tokens), 1)
    square = jnp.sum(jnp.where(at == lane, row, 0.0), axis=1, keepdims=True)
    out[...] = (wide * lax.rsqrt(square / D + EPS) * gain[...]).astype(jnp.bfloat16)


def small_call(kernel, shape, dtype, *operands):
    return pl.pallas_call(
        kernel,
        out_shape=jax.ShapeDtypeStruct(shape, dtype),
        in_specs=[pl.BlockSpec(memory_space=pltpu.VMEM)] * len(operands),
        out_specs=pl.BlockSpec(memory_space=pltpu.VMEM),
        compiler_params=pltpu.CompilerParams(vmem_limit_bytes=8 * 1024 * 1024),
    )(*operands)


def key_row(position):
    step, at = divmod(position, PIECE)
    return step * (PIECE + VALUE_ROWS * (PIECE // LANES)) + at


def value_row(position):
    step, at = divmod(position, PIECE)
    return key_row(step * PIECE) + PIECE + at // LANES * VALUE_ROWS


def prepare_kernel(length, keys, values, out):
    count = keys.shape[0]
    valid = length[0]
    at = lax.broadcasted_iota(jnp.int32, (HD, HD), 0)
    lane = lax.broadcasted_iota(jnp.int32, (HD, HD), 1)
    unit = jnp.where(at == lane, 1.0, 0.0).astype(jnp.bfloat16)

    def write(masked):
        for start in range(0, count, PIECE):
            own_keys = keys[start : start + PIECE, :]
            own_values = values[start : start + PIECE, :]
            if masked:
                inside = start + lax.broadcasted_iota(jnp.int32, (PIECE, HD), 0) < valid
                first = keys[0:16, :].astype(jnp.float32)[0:1, :]
                own_keys = jnp.where(inside, own_keys.astype(jnp.float32), first)
                own_keys = own_keys.astype(jnp.bfloat16)
                own_values = jnp.where(inside, own_values.astype(jnp.float32), 0.0)
                own_values = own_values.astype(jnp.bfloat16)
            out[key_row(start) : key_row(start) + PIECE, :] = own_keys
            across = lax.dot_general(
                unit, own_values, (((1,), (1,)), ((), ())), preferred_element_type=jnp.float32
            ).astype(jnp.bfloat16)
            for block in range(0, PIECE, LANES):
                row = value_row(start + block)
                out[row : row + HD, :] = across[:, block : block + LANES]
                ones = jnp.ones((ONES_ROWS, LANES), jnp.float32)
                if masked:
                    place = lax.broadcasted_iota(jnp.int32, (ONES_ROWS, LANES), 1)
                    ones = jnp.where(start + block + place < valid, ones, 0.0)
                out[row + HD : row + VALUE_ROWS, :] = ones.astype(jnp.bfloat16)

    pl.when(valid >= count)(functools.partial(write, False))
    pl.when(valid < count)(functools.partial(write, True))


def prepare(lengths, keys, values):
    count = keys.shape[0]
    return pl.pallas_call(
        prepare_kernel,
        out_shape=jax.ShapeDtypeStruct((key_row(count), HD), jnp.bfloat16),
        in_specs=[
            pl.BlockSpec(memory_space=pltpu.SMEM),
            pl.BlockSpec(memory_space=pltpu.VMEM),
            pl.BlockSpec(memory_space=pltpu.VMEM),
        ],
        out_specs=pl.BlockSpec(memory_space=pltpu.VMEM),
        compiler_params=pltpu.CompilerParams(vmem_limit_bytes=16 * 1024 * 1024),
        cost_estimate=pl.CostEstimate(
            flops=8 * count * HD, bytes_accessed=8 * count * HD, transcendentals=0
        ),
    )(lengths, keys, values)


def attend_kernel(query, here, there, out, scores, *, chunks, count):
    tokens = query.shape[0]
    wide = 2 * tokens
    cache = (here, there)
    reach = scores.shape[1]
    pairs = OWN // 2
    unit = math.log2(math.e) / math.sqrt(HD)
    units = [
        (half, start, pair)
        for half in range(CORES)
        for start in range(0, count, reach)
        for pair in range(pairs)
    ]

    def query_pair(pair):
        base = pair * 2 * HD
        return jnp.concatenate(
            [query[:, base : base + HD], query[:, base + HD : base + 2 * HD]], axis=0
        )

    queries = [query_pair(pair) for pair in range(pairs)]

    def score_piece(number, offset, top):
        half, start, pair = units[number]
        row = key_row(start + offset)
        part = lax.dot_general(
            cache[half][row : row + PIECE, :],
            queries[pair],
            (((1,), (1,)), ((), ())),
            preferred_element_type=jnp.float32,
        )
        scores[number % 2, offset : offset + PIECE, :] = part
        return jnp.maximum(top, jnp.max(part.reshape(PIECE // 8, 8, wide), axis=0))

    lowest = jnp.full((8, wide), -jnp.inf, jnp.float32)
    top = lowest
    for offset in range(0, reach, PIECE):
        top = score_piece(0, offset, top)
    held = [None] * pairs
    for number, (half, start, pair) in enumerate(units):
        best = jnp.max(top, axis=0, keepdims=True)
        top = lowest
        accum = jnp.zeros((VALUE_ROWS, wide), jnp.float32)
        for offset in range(0, reach, PIECE):
            if number + 1 < len(units):
                top = score_piece(number + 1, offset, top)
            weight = jnp.exp2((scores[number % 2, offset : offset + PIECE, :] - best) * unit)
            across = [
                cache[half][value_row(at) : value_row(at) + VALUE_ROWS, :]
                for at in range(start + offset, start + offset + PIECE, LANES)
            ]
            accum += jnp.dot(
                jnp.concatenate(across, axis=1),
                weight.astype(jnp.bfloat16),
                preferred_element_type=jnp.float32,
            )
        if held[pair] is not None:
            before, summed = held[pair]
            both = jnp.maximum(before, best)
            accum = summed * jnp.exp2((before - both) * unit) + accum * jnp.exp2(
                (best - both) * unit
            )
            best = both
        held[pair] = (best, accum)

    for pair in range(pairs):
        best, accum = held[pair]
        total = accum[HD : HD + 1, :]
        level = best * unit + jnp.log2(total)
        high = jnp.where(jnp.abs(level) < 1.0, 0.0, level).astype(jnp.bfloat16).astype(jnp.float32)
        rest = level - high
        middle = rest.astype(jnp.bfloat16).astype(jnp.float32)
        stats = jnp.concatenate(
            [
                high * (1.0 / LEVEL_STEP),
                middle,
                (rest - middle) * LEVEL_STEP,
                jnp.zeros((STAT_ROWS - 3, wide), jnp.float32),
            ],
            axis=0,
        )
        mean = accum[0:HD, :] * (ACCUM_SCALE / total)
        per_head = chunks // OWN
        rows = HD // per_head
        for side in range(2):
            lanes = slice(side * tokens, (side + 1) * tokens)
            for part in range(per_head):
                chunk = (2 * pair + side) * per_head + part
                out[chunk, 0:rows, :] = mean[part * rows : (part + 1) * rows, lanes]
                out[chunk, rows : rows + STAT_ROWS, :] = stats[:, lanes]


def attend(query, here, there, count, chunks):
    tokens = query.shape[0]
    rows = OWN * HD // chunks
    return pl.pallas_call(
        functools.partial(attend_kernel, chunks=chunks, count=count),
        out_shape=jax.ShapeDtypeStruct((chunks, rows + STAT_ROWS, tokens), jnp.float32),
        in_specs=[pl.BlockSpec(memory_space=pltpu.VMEM)] * 3,
        out_specs=pl.BlockSpec(memory_space=pltpu.VMEM),
        scratch_shapes=[pltpu.VMEM((2, min(count, REACH), 2 * tokens), jnp.float32)],
        compiler_params=pltpu.CompilerParams(vmem_limit_bytes=24 * 1024 * 1024),
        cost_estimate=pl.CostEstimate(
            flops=4 * GROUP * tokens * count * HD,
            bytes_accessed=8 * count * HD,
            transcendentals=GROUP * tokens * count,
        ),
    )(query, here, there)


def local(span, gain, w_query, keys, values, lengths, w_out):
    chips = lax.axis_size("z")
    shards = CORES * chips
    heads = lax.axis_size("tp")
    own = span[0]
    step = own.shape[0]
    tokens = heads * step
    width = GROUP * HD

    here = prepare(lengths, keys[0, :, 0, :], values[0, :, 0, :])
    span_rows = spread(own, "tp").reshape(tokens, -1)
    span_rows, here = lax.optimization_barrier((span_rows, here))
    there = from_behind(here, "core", 1)

    squares = small_call(square_kernel, (shards, 1, tokens), jnp.float32, span_rows)
    squares = lax.all_to_all(squares, ("core", "z"), 0, 0)
    normed = small_call(norm_kernel, span_rows.shape, jnp.bfloat16, squares, span_rows, gain)
    partial = jnp.dot(normed, w_query[0], preferred_element_type=jnp.float32) * QUERY_SCALE
    partial = partial.astype(jnp.float16).reshape(tokens, CORES, width // CORES)
    partial = jnp.swapaxes(partial, 0, 1).reshape(shards, tokens // chips, width // CORES)
    parts = lax.all_to_all(partial, ("core", "z"), 0, 0)
    query = jnp.sum(parts.astype(jnp.float32), axis=0) * (1.0 / QUERY_SCALE)
    query = spread(query.astype(jnp.bfloat16), "z").reshape(tokens, width // CORES)

    rows = width // shards
    pieces = attend(query, here, there, keys.shape[1], chips).astype(jnp.float16)
    pieces = lax.all_to_all(pieces, "z", 0, 0).astype(jnp.float32)
    level = (
        pieces[:, rows, :] * LEVEL_STEP
        + pieces[:, rows + 1, :]
        + pieces[:, rows + 2, :] * (1.0 / LEVEL_STEP)
    )
    factor = jnp.exp2(level - jnp.max(level, axis=0, keepdims=True))
    numer = jnp.sum(pieces[:, :rows, :] * factor[:, None, :], axis=0)
    denom = jnp.sum(factor, axis=0, keepdims=True) * ACCUM_SCALE
    attended = spread((numer / denom).astype(jnp.bfloat16), ("core", "z")).reshape(width, tokens)

    projected = lax.dot_general(
        attended, w_out[0], (((0,), (0,)), ((), ())), preferred_element_type=jnp.float32
    )
    projected = (projected * OUT_SCALE).astype(jnp.float16).reshape(heads, step, -1)
    parts = lax.all_to_all(projected, "tp", 0, 0).astype(jnp.float32)
    updated = (own.astype(jnp.float32) + jnp.sum(parts, axis=0) * (1.0 / OUT_SCALE)).astype(jnp.bfloat16)
    return from_behind(updated, "section", 1)[None]


def solution(mesh):
    shards, sections, heads = (mesh.shape[name] for name in ("kvp", "section", "tp"))
    split = Mesh(
        mesh.devices.reshape(shards // CORES, CORES, sections, heads),
        ("z", "core", "section", "tp"),
    )
    shard = ("z", "core")
    in_specs = (
        P("section", "tp", shard),
        P("section", shard),
        P("section", shard, "tp"),
        P("section", shard, "tp", None),
        P("section", shard, "tp", None),
        P(shard),
        P("section", "tp", shard),
    )
    out_specs = P("section", "tp", shard)
    return jax.shard_map(local, mesh=split, in_specs=in_specs, out_specs=out_specs, check_vma=False)
```

```python
import functools
import math

import jax
import jax.numpy as jnp
from jax import lax
from jax.experimental import pallas as pl
from jax.experimental.pallas import tpu as pltpu
from jax.sharding import Mesh, PartitionSpec as P

D = 8192
HEADS = 64
KV_HEADS = 8
HD = 128
EPS = 1e-05

GROUP = HEADS // KV_HEADS
CORES = 2
OWN = GROUP // CORES
LANES = 128
STAT_ROWS = 8
ONES_ROWS = 16
VALUE_ROWS = HD + ONES_ROWS
PIECE = 2048
REACH = 2048

QUERY_SCALE = 128.0
ACCUM_SCALE = 4096.0
OUT_SCALE = 64.0
LEVEL_STEP = 256.0

def from_behind(value, axis, steps):
    count = lax.axis_size(axis)
    pairs = [(source, (source + steps) % count) for source in range(count)]
    return lax.ppermute(value, axis, pairs)


def spread(value, axis):
    count = lax.psum(1, axis)
    return lax.all_to_all(jnp.broadcast_to(value[None], (count,) + value.shape), axis, 0, 0)


def square_kernel(rows, out):
    wide = rows[...].astype(jnp.float32)
    square = jnp.sum(wide * wide, axis=1, keepdims=True)
    tokens = wide.shape[0]
    at = lax.broadcasted_iota(jnp.int32, (tokens, tokens), 0)
    lane = lax.broadcasted_iota(jnp.int32, (tokens, tokens), 1)
    row = jnp.sum(jnp.where(at == lane, square, 0.0), axis=0, keepdims=True)
    out[...] = jnp.broadcast_to(row[None], out.shape)


def norm_kernel(squares, rows, gain, out):
    wide = rows[...].astype(jnp.float32)
    tokens = wide.shape[0]
    row = jnp.sum(squares[...], axis=0)
    at = lax.broadcasted_iota(jnp.int32, (tokens, tokens), 0)
    lane = lax.broadcasted_iota(jnp.int32, (tokens, tokens), 1)
    square = jnp.sum(jnp.where(at == lane, row, 0.0), axis=1, keepdims=True)
    out[...] = (wide * lax.rsqrt(square / D + EPS) * gain[...]).astype(jnp.bfloat16)


def small_call(kernel, shape, dtype, *operands):
    return pl.pallas_call(
        kernel,
        out_shape=jax.ShapeDtypeStruct(shape, dtype),
        in_specs=[pl.BlockSpec(memory_space=pltpu.VMEM)] * len(operands),
        out_specs=pl.BlockSpec(memory_space=pltpu.VMEM),
        compiler_params=pltpu.CompilerParams(vmem_limit_bytes=8 * 1024 * 1024),
    )(*operands)


def key_row(position):
    step, at = divmod(position, PIECE)
    return step * (PIECE + VALUE_ROWS * (PIECE // LANES)) + at


def value_row(position):
    step, at = divmod(position, PIECE)
    return key_row(step * PIECE) + PIECE + at // LANES * VALUE_ROWS


def prepare_kernel(length, keys, values, out):
    count = keys.shape[0]
    valid = length[0]
    at = lax.broadcasted_iota(jnp.int32, (HD, HD), 0)
    lane = lax.broadcasted_iota(jnp.int32, (HD, HD), 1)
    unit = jnp.where(at == lane, 1.0, 0.0).astype(jnp.bfloat16)

    def write(masked):
        for start in range(0, count, PIECE):
            own_keys = keys[start : start + PIECE, :]
            own_values = values[start : start + PIECE, :]
            if masked:
                inside = start + lax.broadcasted_iota(jnp.int32, (PIECE, HD), 0) < valid
                first = keys[0:16, :].astype(jnp.float32)[0:1, :]
                own_keys = jnp.where(inside, own_keys.astype(jnp.float32), first)
                own_keys = own_keys.astype(jnp.bfloat16)
                own_values = jnp.where(inside, own_values.astype(jnp.float32), 0.0)
                own_values = own_values.astype(jnp.bfloat16)
            out[key_row(start) : key_row(start) + PIECE, :] = own_keys
            across = lax.dot_general(
                unit, own_values, (((1,), (1,)), ((), ())), preferred_element_type=jnp.float32
            ).astype(jnp.bfloat16)
            for block in range(0, PIECE, LANES):
                row = value_row(start + block)
                out[row : row + HD, :] = across[:, block : block + LANES]
                ones = jnp.ones((ONES_ROWS, LANES), jnp.float32)
                if masked:
                    place = lax.broadcasted_iota(jnp.int32, (ONES_ROWS, LANES), 1)
                    ones = jnp.where(start + block + place < valid, ones, 0.0)
                out[row + HD : row + VALUE_ROWS, :] = ones.astype(jnp.bfloat16)

    pl.when(valid >= count)(functools.partial(write, False))
    pl.when(valid < count)(functools.partial(write, True))


def prepare(lengths, keys, values):
    count = keys.shape[0]
    return pl.pallas_call(
        prepare_kernel,
        out_shape=jax.ShapeDtypeStruct((key_row(count), HD), jnp.bfloat16),
        in_specs=[
            pl.BlockSpec(memory_space=pltpu.SMEM),
            pl.BlockSpec(memory_space=pltpu.VMEM),
            pl.BlockSpec(memory_space=pltpu.VMEM),
        ],
        out_specs=pl.BlockSpec(memory_space=pltpu.VMEM),
        compiler_params=pltpu.CompilerParams(vmem_limit_bytes=16 * 1024 * 1024),
        cost_estimate=pl.CostEstimate(
            flops=8 * count * HD, bytes_accessed=8 * count * HD, transcendentals=0
        ),
    )(lengths, keys, values)


def attend_kernel(query, here, there, out, scores, *, chunks, count):
    tokens = query.shape[0]
    wide = 2 * tokens
    cache = (here, there)
    reach = scores.shape[1]
    pairs = OWN // 2
    unit = math.log2(math.e) / math.sqrt(HD)
    units = [
        (half, start, pair)
        for half in range(CORES)
        for start in range(0, count, reach)
        for pair in range(pairs)
    ]

    def query_pair(pair):
        base = pair * 2 * HD
        return jnp.concatenate(
            [query[:, base : base + HD], query[:, base + HD : base + 2 * HD]], axis=0
        )

    queries = [query_pair(pair) for pair in range(pairs)]

    def score_piece(number, offset, top):
        half, start, pair = units[number]
        row = key_row(start + offset)
        part = lax.dot_general(
            cache[half][row : row + PIECE, :],
            queries[pair],
            (((1,), (1,)), ((), ())),
            preferred_element_type=jnp.float32,
        )
        scores[number % 2, offset : offset + PIECE, :] = part
        return jnp.maximum(top, jnp.max(part.reshape(PIECE // 8, 8, wide), axis=0))

    lowest = jnp.full((8, wide), -jnp.inf, jnp.float32)
    top = lowest
    for offset in range(0, reach, PIECE):
        top = score_piece(0, offset, top)
    held = [None] * pairs
    for number, (half, start, pair) in enumerate(units):
        best = jnp.max(top, axis=0, keepdims=True)
        top = lowest
        accum = jnp.zeros((VALUE_ROWS, wide), jnp.float32)
        for offset in range(0, reach, PIECE):
            if number + 1 < len(units):
                top = score_piece(number + 1, offset, top)
            weight = jnp.exp2((scores[number % 2, offset : offset + PIECE, :] - best) * unit)
            across = [
                cache[half][value_row(at) : value_row(at) + VALUE_ROWS, :]
                for at in range(start + offset, start + offset + PIECE, LANES)
            ]
            accum += jnp.dot(
                jnp.concatenate(across, axis=1),
                weight.astype(jnp.bfloat16),
                preferred_element_type=jnp.float32,
            )
        if held[pair] is not None:
            before, summed = held[pair]
            both = jnp.maximum(before, best)
            accum = summed * jnp.exp2((before - both) * unit) + accum * jnp.exp2(
                (best - both) * unit
            )
            best = both
        held[pair] = (best, accum)

    for pair in range(pairs):
        best, accum = held[pair]
        total = accum[HD : HD + 1, :]
        level = best * unit + jnp.log2(total)
        high = jnp.where(jnp.abs(level) < 1.0, 0.0, level).astype(jnp.bfloat16).astype(jnp.float32)
        rest = level - high
        middle = rest.astype(jnp.bfloat16).astype(jnp.float32)
        stats = jnp.concatenate(
            [
                high * (1.0 / LEVEL_STEP),
                middle,
                (rest - middle) * LEVEL_STEP,
                jnp.zeros((STAT_ROWS - 3, wide), jnp.float32),
            ],
            axis=0,
        )
        mean = accum[0:HD, :] * (ACCUM_SCALE / total)
        per_head = chunks // OWN
        rows = HD // per_head
        for side in range(2):
            lanes = slice(side * tokens, (side + 1) * tokens)
            for part in range(per_head):
                chunk = (2 * pair + side) * per_head + part
                out[chunk, 0:rows, :] = mean[part * rows : (part + 1) * rows, lanes]
                out[chunk, rows : rows + STAT_ROWS, :] = stats[:, lanes]


def attend(query, here, there, count, chunks):
    tokens = query.shape[0]
    rows = OWN * HD // chunks
    return pl.pallas_call(
        functools.partial(attend_kernel, chunks=chunks, count=count),
        out_shape=jax.ShapeDtypeStruct((chunks, rows + STAT_ROWS, tokens), jnp.float32),
        in_specs=[pl.BlockSpec(memory_space=pltpu.VMEM)] * 3,
        out_specs=pl.BlockSpec(memory_space=pltpu.VMEM),
        scratch_shapes=[pltpu.VMEM((2, min(count, REACH), 2 * tokens), jnp.float32)],
        compiler_params=pltpu.CompilerParams(vmem_limit_bytes=24 * 1024 * 1024),
        cost_estimate=pl.CostEstimate(
            flops=4 * GROUP * tokens * count * HD,
            bytes_accessed=8 * count * HD,
            transcendentals=GROUP * tokens * count,
        ),
    )(query, here, there)


def local(span, gain, w_query, keys, values, lengths, w_out):
    chips = lax.axis_size("z")
    shards = CORES * chips
    heads = lax.axis_size("tp")
    own = span[0]
    step = own.shape[0]
    tokens = heads * step
    width = GROUP * HD

    here = prepare(lengths, keys[0, :, 0, :], values[0, :, 0, :])
    span_rows = spread(own, "tp").reshape(tokens, -1)
    span_rows, here = lax.optimization_barrier((span_rows, here))
    there = from_behind(here, "core", 1)

    squares = small_call(square_kernel, (shards, 1, tokens), jnp.float32, span_rows)
    squares = lax.all_to_all(squares, ("core", "z"), 0, 0)
    normed = small_call(norm_kernel, span_rows.shape, jnp.bfloat16, squares, span_rows, gain)
    partial = jnp.dot(normed, w_query[0], preferred_element_type=jnp.float32) * QUERY_SCALE
    partial = partial.astype(jnp.float16).reshape(tokens, CORES, width // CORES)
    partial = jnp.swapaxes(partial, 0, 1).reshape(shards, tokens // chips, width // CORES)
    parts = lax.all_to_all(partial, ("core", "z"), 0, 0)
    query = jnp.sum(parts.astype(jnp.float32), axis=0) * (1.0 / QUERY_SCALE)
    query = spread(query.astype(jnp.bfloat16), "z").reshape(tokens, width // CORES)

    rows = width // shards
    pieces = attend(query, here, there, keys.shape[1], chips).astype(jnp.float16)
    pieces = lax.all_to_all(pieces, "z", 0, 0).astype(jnp.float32)
    level = (
        pieces[:, rows, :] * LEVEL_STEP
        + pieces[:, rows + 1, :]
        + pieces[:, rows + 2, :] * (1.0 / LEVEL_STEP)
    )
    factor = jnp.exp2(level - jnp.max(level, axis=0, keepdims=True))
    numer = jnp.sum(pieces[:, :rows, :] * factor[:, None, :], axis=0)
    denom = jnp.sum(factor, axis=0, keepdims=True) * ACCUM_SCALE
    attended = spread((numer / denom).astype(jnp.bfloat16), ("core", "z")).reshape(width, tokens)

    projected = lax.dot_general(
        attended, w_out[0], (((0,), (0,)), ((), ())), preferred_element_type=jnp.float32
    )
    projected = (projected * OUT_SCALE).astype(jnp.float16).reshape(heads, step, -1)
    parts = lax.all_to_all(projected, "tp", 0, 0).astype(jnp.float32)
    updated = (own.astype(jnp.float32) + jnp.sum(parts, axis=0) * (1.0 / OUT_SCALE)).astype(jnp.bfloat16)
    return from_behind(updated, "section", 1)[None]


def solution(mesh):
    shards, sections, heads = (mesh.shape[name] for name in ("kvp", "section", "tp"))
    split = Mesh(
        mesh.devices.reshape(shards // CORES, CORES, sections, heads),
        ("z", "core", "section", "tp"),
    )
    shard = ("z", "core")
    in_specs = (
        P("section", "tp", shard),
        P("section", shard),
        P("section", shard, "tp"),
        P("section", shard, "tp", None),
        P("section", shard, "tp", None),
        P(shard),
        P("section", "tp", shard),
    )
    out_specs = P("section", "tp", shard)
    return jax.shard_map(local, mesh=split, in_specs=in_specs, out_specs=out_specs, check_vma=False)
```

```python
import functools
import math

import jax
import jax.numpy as jnp
from jax import lax
from jax.experimental import pallas as pl
from jax.experimental.pallas import tpu as pltpu
from jax.sharding import Mesh, PartitionSpec as P

D = 8192
HEADS = 64
KV_HEADS = 8
HD = 128
EPS = 1e-05

GROUP = HEADS // KV_HEADS
CORES = 2
OWN = GROUP // CORES
LANES = 128
STAT_ROWS = 8
ONES_ROWS = 16
VALUE_ROWS = HD + ONES_ROWS
PIECE = 1024
REACH = 2048

QUERY_SCALE = 128.0
ACCUM_SCALE = 4096.0
OUT_SCALE = 64.0
LEVEL_STEP = 256.0

def from_behind(value, axis, steps):
    count = lax.axis_size(axis)
    pairs = [(source, (source + steps) % count) for source in range(count)]
    return lax.ppermute(value, axis, pairs)


def spread(value, axis):
    count = lax.psum(1, axis)
    return lax.all_to_all(jnp.broadcast_to(value[None], (count,) + value.shape), axis, 0, 0)


def square_kernel(rows, out):
    wide = rows[...].astype(jnp.float32)
    square = jnp.sum(wide * wide, axis=1, keepdims=True)
    tokens = wide.shape[0]
    at = lax.broadcasted_iota(jnp.int32, (tokens, tokens), 0)
    lane = lax.broadcasted_iota(jnp.int32, (tokens, tokens), 1)
    row = jnp.sum(jnp.where(at == lane, square, 0.0), axis=0, keepdims=True)
    out[...] = jnp.broadcast_to(row[None], out.shape)


def norm_kernel(squares, rows, gain, out):
    wide = rows[...].astype(jnp.float32)
    tokens = wide.shape[0]
    row = jnp.sum(squares[...], axis=0)
    at = lax.broadcasted_iota(jnp.int32, (tokens, tokens), 0)
    lane = lax.broadcasted_iota(jnp.int32, (tokens, tokens), 1)
    square = jnp.sum(jnp.where(at == lane, row, 0.0), axis=1, keepdims=True)
    out[...] = (wide * lax.rsqrt(square / D + EPS) * gain[...]).astype(jnp.bfloat16)


def small_call(kernel, shape, dtype, *operands):
    return pl.pallas_call(
        kernel,
        out_shape=jax.ShapeDtypeStruct(shape, dtype),
        in_specs=[pl.BlockSpec(memory_space=pltpu.VMEM)] * len(operands),
        out_specs=pl.BlockSpec(memory_space=pltpu.VMEM),
        compiler_params=pltpu.CompilerParams(vmem_limit_bytes=8 * 1024 * 1024),
    )(*operands)


def key_row(position):
    step, at = divmod(position, PIECE)
    return step * (PIECE + VALUE_ROWS * (PIECE // LANES)) + at


def value_row(position):
    step, at = divmod(position, PIECE)
    return key_row(step * PIECE) + PIECE + at // LANES * VALUE_ROWS


def prepare_kernel(length, keys, values, out):
    count = keys.shape[0]
    valid = length[0]
    at = lax.broadcasted_iota(jnp.int32, (HD, HD), 0)
    lane = lax.broadcasted_iota(jnp.int32, (HD, HD), 1)
    unit = jnp.where(at == lane, 1.0, 0.0).astype(jnp.bfloat16)

    def write(masked):
        for start in range(0, count, PIECE):
            own_keys = keys[start : start + PIECE, :]
            own_values = values[start : start + PIECE, :]
            if masked:
                inside = start + lax.broadcasted_iota(jnp.int32, (PIECE, HD), 0) < valid
                first = keys[0:16, :].astype(jnp.float32)[0:1, :]
                own_keys = jnp.where(inside, own_keys.astype(jnp.float32), first)
                own_keys = own_keys.astype(jnp.bfloat16)
                own_values = jnp.where(inside, own_values.astype(jnp.float32), 0.0)
                own_values = own_values.astype(jnp.bfloat16)
            out[key_row(start) : key_row(start) + PIECE, :] = own_keys
            across = lax.dot_general(
                unit, own_values, (((1,), (1,)), ((), ())), preferred_element_type=jnp.float32
            ).astype(jnp.bfloat16)
            for block in range(0, PIECE, LANES):
                row = value_row(start + block)
                out[row : row + HD, :] = across[:, block : block + LANES]
                ones = jnp.ones((ONES_ROWS, LANES), jnp.float32)
                if masked:
                    place = lax.broadcasted_iota(jnp.int32, (ONES_ROWS, LANES), 1)
                    ones = jnp.where(start + block + place < valid, ones, 0.0)
                out[row + HD : row + VALUE_ROWS, :] = ones.astype(jnp.bfloat16)

    pl.when(valid >= count)(functools.partial(write, False))
    pl.when(valid < count)(functools.partial(write, True))


def prepare(lengths, keys, values):
    count = keys.shape[0]
    return pl.pallas_call(
        prepare_kernel,
        out_shape=jax.ShapeDtypeStruct((key_row(count), HD), jnp.bfloat16),
        in_specs=[
            pl.BlockSpec(memory_space=pltpu.SMEM),
            pl.BlockSpec(memory_space=pltpu.VMEM),
            pl.BlockSpec(memory_space=pltpu.VMEM),
        ],
        out_specs=pl.BlockSpec(memory_space=pltpu.VMEM),
        compiler_params=pltpu.CompilerParams(vmem_limit_bytes=16 * 1024 * 1024),
        cost_estimate=pl.CostEstimate(
            flops=8 * count * HD, bytes_accessed=8 * count * HD, transcendentals=0
        ),
    )(lengths, keys, values)


def attend_kernel(query, here, there, out, scores, *, chunks, count):
    tokens = query.shape[0]
    wide = 2 * tokens
    cache = (here, there)
    reach = scores.shape[1]
    pairs = OWN // 2
    unit = math.log2(math.e) / math.sqrt(HD)
    units = [
        (half, start, pair)
        for half in range(CORES)
        for start in range(0, count, reach)
        for pair in range(pairs)
    ]

    def query_pair(pair):
        base = pair * 2 * HD
        return jnp.concatenate(
            [query[:, base : base + HD], query[:, base + HD : base + 2 * HD]], axis=0
        )

    queries = [query_pair(pair) for pair in range(pairs)]

    def score_piece(number, offset, top):
        half, start, pair = units[number]
        row = key_row(start + offset)
        part = lax.dot_general(
            cache[half][row : row + PIECE, :],
            queries[pair],
            (((1,), (1,)), ((), ())),
            preferred_element_type=jnp.float32,
        )
        scores[number % 2, offset : offset + PIECE, :] = part
        return jnp.maximum(top, jnp.max(part.reshape(PIECE // 8, 8, wide), axis=0))

    lowest = jnp.full((8, wide), -jnp.inf, jnp.float32)
    top = lowest
    for offset in range(0, reach, PIECE):
        top = score_piece(0, offset, top)
    held = [None] * pairs
    for number, (half, start, pair) in enumerate(units):
        best = jnp.max(top, axis=0, keepdims=True)
        top = lowest
        accum = None
        if held[pair] is not None:
            before, accum = held[pair]
            best = jnp.maximum(before, best)
            accum = accum * jnp.exp2((before - best) * unit)
        for offset in range(0, reach, PIECE):
            if number + 1 < len(units):
                top = score_piece(number + 1, offset, top)
            weight = jnp.exp2((scores[number % 2, offset : offset + PIECE, :] - best) * unit)
            across = [
                cache[half][value_row(at) : value_row(at) + VALUE_ROWS, :]
                for at in range(start + offset, start + offset + PIECE, LANES)
            ]
            product = jnp.dot(
                jnp.concatenate(across, axis=1),
                weight.astype(jnp.bfloat16),
                preferred_element_type=jnp.float32,
            )
            accum = product if accum is None else accum + product
        held[pair] = (best, accum)

    for pair in range(pairs):
        best, accum = held[pair]
        total = accum[HD : HD + 1, :]
        level = best * unit + jnp.log2(total)
        high = jnp.where(jnp.abs(level) < 1.0, 0.0, level).astype(jnp.bfloat16).astype(jnp.float32)
        rest = level - high
        middle = rest.astype(jnp.bfloat16).astype(jnp.float32)
        stats = jnp.concatenate(
            [
                high * (1.0 / LEVEL_STEP),
                middle,
                (rest - middle) * LEVEL_STEP,
                jnp.zeros((STAT_ROWS - 3, wide), jnp.float32),
            ],
            axis=0,
        )
        mean = accum[0:HD, :] * (ACCUM_SCALE / total)
        per_head = chunks // OWN
        rows = HD // per_head
        for side in range(2):
            lanes = slice(side * tokens, (side + 1) * tokens)
            for part in range(per_head):
                chunk = (2 * pair + side) * per_head + part
                out[chunk, 0:rows, :] = mean[part * rows : (part + 1) * rows, lanes]
                out[chunk, rows : rows + STAT_ROWS, :] = stats[:, lanes]


def attend(query, here, there, count, chunks):
    tokens = query.shape[0]
    rows = OWN * HD // chunks
    return pl.pallas_call(
        functools.partial(attend_kernel, chunks=chunks, count=count),
        out_shape=jax.ShapeDtypeStruct((chunks, rows + STAT_ROWS, tokens), jnp.float32),
        in_specs=[pl.BlockSpec(memory_space=pltpu.VMEM)] * 3,
        out_specs=pl.BlockSpec(memory_space=pltpu.VMEM),
        scratch_shapes=[pltpu.VMEM((2, min(count, REACH), 2 * tokens), jnp.float32)],
        compiler_params=pltpu.CompilerParams(vmem_limit_bytes=24 * 1024 * 1024),
        cost_estimate=pl.CostEstimate(
            flops=4 * GROUP * tokens * count * HD,
            bytes_accessed=8 * count * HD,
            transcendentals=GROUP * tokens * count,
        ),
    )(query, here, there)


def local(span, gain, w_query, keys, values, lengths, w_out):
    chips = lax.axis_size("z")
    shards = CORES * chips
    heads = lax.axis_size("tp")
    own = span[0]
    step = own.shape[0]
    tokens = heads * step
    width = GROUP * HD

    here = prepare(lengths, keys[0, :, 0, :], values[0, :, 0, :])
    span_rows = spread(own, "tp").reshape(tokens, -1)
    span_rows, here = lax.optimization_barrier((span_rows, here))
    there = from_behind(here, "core", 1)

    squares = small_call(square_kernel, (shards, 1, tokens), jnp.float32, span_rows)
    squares = lax.all_to_all(squares, ("core", "z"), 0, 0)
    normed = small_call(norm_kernel, span_rows.shape, jnp.bfloat16, squares, span_rows, gain)
    partial = jnp.dot(normed, w_query[0], preferred_element_type=jnp.float32) * QUERY_SCALE
    partial = partial.astype(jnp.float16).reshape(tokens, CORES, width // CORES)
    partial = jnp.swapaxes(partial, 0, 1).reshape(shards, tokens // chips, width // CORES)
    parts = lax.all_to_all(partial, ("core", "z"), 0, 0)
    query = jnp.sum(parts.astype(jnp.float32), axis=0) * (1.0 / QUERY_SCALE)
    query = spread(query.astype(jnp.bfloat16), "z").reshape(tokens, width // CORES)

    rows = width // shards
    pieces = attend(query, here, there, keys.shape[1], chips).astype(jnp.float16)
    pieces = lax.all_to_all(pieces, "z", 0, 0).astype(jnp.float32)
    level = (
        pieces[:, rows, :] * LEVEL_STEP
        + pieces[:, rows + 1, :]
        + pieces[:, rows + 2, :] * (1.0 / LEVEL_STEP)
    )
    factor = jnp.exp2(level - jnp.max(level, axis=0, keepdims=True))
    numer = jnp.sum(pieces[:, :rows, :] * factor[:, None, :], axis=0)
    denom = jnp.sum(factor, axis=0, keepdims=True) * ACCUM_SCALE
    attended = spread((numer / denom).astype(jnp.bfloat16), ("core", "z")).reshape(width, tokens)

    projected = lax.dot_general(
        attended, w_out[0], (((0,), (0,)), ((), ())), preferred_element_type=jnp.float32
    )
    projected = (projected * OUT_SCALE).astype(jnp.float16).reshape(heads, step, -1)
    parts = lax.all_to_all(projected, "tp", 0, 0).astype(jnp.float32)
    updated = (own.astype(jnp.float32) + jnp.sum(parts, axis=0) * (1.0 / OUT_SCALE)).astype(jnp.bfloat16)
    return from_behind(updated, "section", 1)[None]


def solution(mesh):
    shards, sections, heads = (mesh.shape[name] for name in ("kvp", "section", "tp"))
    split = Mesh(
        mesh.devices.reshape(shards // CORES, CORES, sections, heads),
        ("z", "core", "section", "tp"),
    )
    shard = ("z", "core")
    in_specs = (
        P("section", "tp", shard),
        P("section", shard),
        P("section", shard, "tp"),
        P("section", shard, "tp", None),
        P("section", shard, "tp", None),
        P(shard),
        P("section", "tp", shard),
    )
    out_specs = P("section", "tp", shard)
    return jax.shard_map(local, mesh=split, in_specs=in_specs, out_specs=out_specs, check_vma=False)
```

```python
import functools
import math

import jax
import jax.numpy as jnp
from jax import lax
from jax.experimental import pallas as pl
from jax.experimental.pallas import tpu as pltpu
from jax.sharding import Mesh, PartitionSpec as P

D = 8192
HEADS = 64
KV_HEADS = 8
HD = 128
EPS = 1e-05

GROUP = HEADS // KV_HEADS
CORES = 2
OWN = GROUP // CORES
LANES = 128
STAT_ROWS = 8
ONES_ROWS = 16
VALUE_ROWS = HD + ONES_ROWS
PIECE = 1024
REACH = 2048

QUERY_SCALE = 128.0
ACCUM_SCALE = 4096.0
OUT_SCALE = 64.0
LEVEL_STEP = 256.0

def from_behind(value, axis, steps):
    count = lax.axis_size(axis)
    pairs = [(source, (source + steps) % count) for source in range(count)]
    return lax.ppermute(value, axis, pairs)


def spread(value, axis):
    count = lax.psum(1, axis)
    return lax.all_to_all(jnp.broadcast_to(value[None], (count,) + value.shape), axis, 0, 0)


def square_kernel(rows, out):
    wide = rows[...].astype(jnp.float32)
    square = jnp.sum(wide * wide, axis=1, keepdims=True)
    tokens = wide.shape[0]
    at = lax.broadcasted_iota(jnp.int32, (tokens, tokens), 0)
    lane = lax.broadcasted_iota(jnp.int32, (tokens, tokens), 1)
    row = jnp.sum(jnp.where(at == lane, square, 0.0), axis=0, keepdims=True)
    out[...] = jnp.broadcast_to(row[None], out.shape)


def norm_kernel(squares, rows, gain, out):
    wide = rows[...].astype(jnp.float32)
    tokens = wide.shape[0]
    row = jnp.sum(squares[...], axis=0)
    at = lax.broadcasted_iota(jnp.int32, (tokens, tokens), 0)
    lane = lax.broadcasted_iota(jnp.int32, (tokens, tokens), 1)
    square = jnp.sum(jnp.where(at == lane, row, 0.0), axis=1, keepdims=True)
    out[...] = (wide * lax.rsqrt(square / D + EPS) * gain[...]).astype(jnp.bfloat16)


def small_call(kernel, shape, dtype, *operands):
    return pl.pallas_call(
        kernel,
        out_shape=jax.ShapeDtypeStruct(shape, dtype),
        in_specs=[pl.BlockSpec(memory_space=pltpu.VMEM)] * len(operands),
        out_specs=pl.BlockSpec(memory_space=pltpu.VMEM),
        compiler_params=pltpu.CompilerParams(vmem_limit_bytes=8 * 1024 * 1024),
    )(*operands)


def key_row(position):
    step, at = divmod(position, PIECE)
    return step * (PIECE + VALUE_ROWS * (PIECE // LANES)) + at


def value_row(position):
    step, at = divmod(position, PIECE)
    return key_row(step * PIECE) + PIECE + at // LANES * VALUE_ROWS


def prepare_kernel(length, keys, values, out):
    count = keys.shape[0]
    valid = length[0]
    at = lax.broadcasted_iota(jnp.int32, (HD, HD), 0)
    lane = lax.broadcasted_iota(jnp.int32, (HD, HD), 1)
    unit = jnp.where(at == lane, 1.0, 0.0).astype(jnp.bfloat16)

    def write(masked):
        for start in range(0, count, PIECE):
            own_keys = keys[start : start + PIECE, :]
            own_values = values[start : start + PIECE, :]
            if masked:
                inside = start + lax.broadcasted_iota(jnp.int32, (PIECE, HD), 0) < valid
                first = keys[0:16, :].astype(jnp.float32)[0:1, :]
                own_keys = jnp.where(inside, own_keys.astype(jnp.float32), first)
                own_keys = own_keys.astype(jnp.bfloat16)
                own_values = jnp.where(inside, own_values.astype(jnp.float32), 0.0)
                own_values = own_values.astype(jnp.bfloat16)
            out[key_row(start) : key_row(start) + PIECE, :] = own_keys
            across = lax.dot_general(
                unit, own_values, (((1,), (1,)), ((), ())), preferred_element_type=jnp.float32
            ).astype(jnp.bfloat16)
            for block in range(0, PIECE, LANES):
                row = value_row(start + block)
                out[row : row + HD, :] = across[:, block : block + LANES]
                ones = jnp.ones((ONES_ROWS, LANES), jnp.float32)
                if masked:
                    place = lax.broadcasted_iota(jnp.int32, (ONES_ROWS, LANES), 1)
                    ones = jnp.where(start + block + place < valid, ones, 0.0)
                out[row + HD : row + VALUE_ROWS, :] = ones.astype(jnp.bfloat16)

    pl.when(valid >= count)(functools.partial(write, False))
    pl.when(valid < count)(functools.partial(write, True))


def prepare(lengths, keys, values):
    count = keys.shape[0]
    return pl.pallas_call(
        prepare_kernel,
        out_shape=jax.ShapeDtypeStruct((key_row(count), HD), jnp.bfloat16),
        in_specs=[
            pl.BlockSpec(memory_space=pltpu.SMEM),
            pl.BlockSpec(memory_space=pltpu.VMEM),
            pl.BlockSpec(memory_space=pltpu.VMEM),
        ],
        out_specs=pl.BlockSpec(memory_space=pltpu.VMEM),
        compiler_params=pltpu.CompilerParams(vmem_limit_bytes=16 * 1024 * 1024),
        cost_estimate=pl.CostEstimate(
            flops=8 * count * HD, bytes_accessed=8 * count * HD, transcendentals=0
        ),
    )(lengths, keys, values)


def attend_kernel(query, here, there, out, scores, *, chunks, count):
    tokens = query.shape[0]
    wide = 2 * tokens
    cache = (here, there)
    reach = scores.shape[1]
    pairs = OWN // 2
    unit = math.log2(math.e) / math.sqrt(HD)
    units = [
        (half, start, pair)
        for half in range(CORES)
        for start in range(0, count, reach)
        for pair in range(pairs)
    ]

    def query_pair(pair):
        base = pair * 2 * HD
        return jnp.concatenate(
            [query[:, base : base + HD], query[:, base + HD : base + 2 * HD]], axis=0
        )

    queries = [query_pair(pair) for pair in range(pairs)]

    def score_piece(number, offset, top):
        half, start, pair = units[number]
        row = key_row(start + offset)
        part = lax.dot_general(
            cache[half][row : row + PIECE, :],
            queries[pair],
            (((1,), (1,)), ((), ())),
            preferred_element_type=jnp.float32,
        )
        scores[number % 2, offset : offset + PIECE, :] = part
        return jnp.maximum(top, jnp.max(part.reshape(PIECE // 8, 8, wide), axis=0))

    lowest = jnp.full((8, wide), -jnp.inf, jnp.float32)
    top = lowest
    for offset in range(0, reach, PIECE):
        top = score_piece(0, offset, top)
    held = [[] for _ in range(pairs)]
    for number, (half, start, pair) in enumerate(units):
        best = jnp.max(top, axis=0, keepdims=True)
        top = lowest
        accum = None
        for offset in range(0, reach, PIECE):
            if number + 1 < len(units):
                top = score_piece(number + 1, offset, top)
            weight = jnp.exp2((scores[number % 2, offset : offset + PIECE, :] - best) * unit)
            across = [
                cache[half][value_row(at) : value_row(at) + VALUE_ROWS, :]
                for at in range(start + offset, start + offset + PIECE, LANES)
            ]
            product = jnp.dot(
                jnp.concatenate(across, axis=1),
                weight.astype(jnp.bfloat16),
                preferred_element_type=jnp.float32,
            )
            accum = product if accum is None else accum + product
        held[pair].append((best, accum))

    for pair in range(pairs):
        best = functools.reduce(jnp.maximum, [own for own, _ in held[pair]])
        accum = sum(part * jnp.exp2((own - best) * unit) for own, part in held[pair])
        total = accum[HD : HD + 1, :]
        level = best * unit + jnp.log2(total)
        high = jnp.where(jnp.abs(level) < 1.0, 0.0, level).astype(jnp.bfloat16).astype(jnp.float32)
        rest = level - high
        middle = rest.astype(jnp.bfloat16).astype(jnp.float32)
        stats = jnp.concatenate(
            [
                high * (1.0 / LEVEL_STEP),
                middle,
                (rest - middle) * LEVEL_STEP,
                jnp.zeros((STAT_ROWS - 3, wide), jnp.float32),
            ],
            axis=0,
        )
        mean = accum[0:HD, :] * (ACCUM_SCALE / total)
        per_head = chunks // OWN
        rows = HD // per_head
        for side in range(2):
            lanes = slice(side * tokens, (side + 1) * tokens)
            for part in range(per_head):
                chunk = (2 * pair + side) * per_head + part
                out[chunk, 0:rows, :] = mean[part * rows : (part + 1) * rows, lanes]
                out[chunk, rows : rows + STAT_ROWS, :] = stats[:, lanes]


def attend(query, here, there, count, chunks):
    tokens = query.shape[0]
    rows = OWN * HD // chunks
    return pl.pallas_call(
        functools.partial(attend_kernel, chunks=chunks, count=count),
        out_shape=jax.ShapeDtypeStruct((chunks, rows + STAT_ROWS, tokens), jnp.float32),
        in_specs=[pl.BlockSpec(memory_space=pltpu.VMEM)] * 3,
        out_specs=pl.BlockSpec(memory_space=pltpu.VMEM),
        scratch_shapes=[pltpu.VMEM((2, min(count, REACH), 2 * tokens), jnp.float32)],
        compiler_params=pltpu.CompilerParams(vmem_limit_bytes=24 * 1024 * 1024),
        cost_estimate=pl.CostEstimate(
            flops=4 * GROUP * tokens * count * HD,
            bytes_accessed=8 * count * HD,
            transcendentals=GROUP * tokens * count,
        ),
    )(query, here, there)


def local(span, gain, w_query, keys, values, lengths, w_out):
    chips = lax.axis_size("z")
    shards = CORES * chips
    heads = lax.axis_size("tp")
    own = span[0]
    step = own.shape[0]
    tokens = heads * step
    width = GROUP * HD

    here = prepare(lengths, keys[0, :, 0, :], values[0, :, 0, :])
    span_rows = spread(own, "tp").reshape(tokens, -1)
    span_rows, here = lax.optimization_barrier((span_rows, here))
    there = from_behind(here, "core", 1)

    squares = small_call(square_kernel, (shards, 1, tokens), jnp.float32, span_rows)
    squares = lax.all_to_all(squares, ("core", "z"), 0, 0)
    normed = small_call(norm_kernel, span_rows.shape, jnp.bfloat16, squares, span_rows, gain)
    partial = jnp.dot(normed, w_query[0], preferred_element_type=jnp.float32) * QUERY_SCALE
    partial = partial.astype(jnp.float16).reshape(tokens, CORES, width // CORES)
    partial = jnp.swapaxes(partial, 0, 1).reshape(shards, tokens // chips, width // CORES)
    parts = lax.all_to_all(partial, ("core", "z"), 0, 0)
    query = jnp.sum(parts.astype(jnp.float32), axis=0) * (1.0 / QUERY_SCALE)
    query = spread(query.astype(jnp.bfloat16), "z").reshape(tokens, width // CORES)

    rows = width // shards
    pieces = attend(query, here, there, keys.shape[1], chips).astype(jnp.float16)
    pieces = lax.all_to_all(pieces, "z", 0, 0).astype(jnp.float32)
    level = (
        pieces[:, rows, :] * LEVEL_STEP
        + pieces[:, rows + 1, :]
        + pieces[:, rows + 2, :] * (1.0 / LEVEL_STEP)
    )
    factor = jnp.exp2(level - jnp.max(level, axis=0, keepdims=True))
    numer = jnp.sum(pieces[:, :rows, :] * factor[:, None, :], axis=0)
    denom = jnp.sum(factor, axis=0, keepdims=True) * ACCUM_SCALE
    attended = spread((numer / denom).astype(jnp.bfloat16), ("core", "z")).reshape(width, tokens)

    projected = lax.dot_general(
        attended, w_out[0], (((0,), (0,)), ((), ())), preferred_element_type=jnp.float32
    )
    projected = (projected * OUT_SCALE).astype(jnp.float16).reshape(heads, step, -1)
    parts = lax.all_to_all(projected, "tp", 0, 0).astype(jnp.float32)
    updated = (own.astype(jnp.float32) + jnp.sum(parts, axis=0) * (1.0 / OUT_SCALE)).astype(jnp.bfloat16)
    return from_behind(updated, "section", 1)[None]


def solution(mesh):
    shards, sections, heads = (mesh.shape[name] for name in ("kvp", "section", "tp"))
    split = Mesh(
        mesh.devices.reshape(shards // CORES, CORES, sections, heads),
        ("z", "core", "section", "tp"),
    )
    shard = ("z", "core")
    in_specs = (
        P("section", "tp", shard),
        P("section", shard),
        P("section", shard, "tp"),
        P("section", shard, "tp", None),
        P("section", shard, "tp", None),
        P(shard),
        P("section", "tp", shard),
    )
    out_specs = P("section", "tp", shard)
    return jax.shard_map(local, mesh=split, in_specs=in_specs, out_specs=out_specs, check_vma=False)
```

```python
import functools
import math

import jax
import jax.numpy as jnp
from jax import lax
from jax.experimental import pallas as pl
from jax.experimental.pallas import tpu as pltpu
from jax.sharding import Mesh, PartitionSpec as P

D = 8192
HEADS = 64
KV_HEADS = 8
HD = 128
EPS = 1e-05

GROUP = HEADS // KV_HEADS
CORES = 2
OWN = GROUP // CORES
LANES = 128
STAT_ROWS = 8
ONES_ROWS = 16
VALUE_ROWS = HD + ONES_ROWS
PIECE = 1024
STEP = PIECE // 2
REACH = 2048

QUERY_SCALE = 128.0
ACCUM_SCALE = 4096.0
OUT_SCALE = 64.0
LEVEL_STEP = 256.0

def from_behind(value, axis, steps):
    count = lax.axis_size(axis)
    pairs = [(source, (source + steps) % count) for source in range(count)]
    return lax.ppermute(value, axis, pairs)


def spread(value, axis):
    count = lax.psum(1, axis)
    return lax.all_to_all(jnp.broadcast_to(value[None], (count,) + value.shape), axis, 0, 0)


def square_kernel(rows, out):
    wide = rows[...].astype(jnp.float32)
    square = jnp.sum(wide * wide, axis=1, keepdims=True)
    tokens = wide.shape[0]
    at = lax.broadcasted_iota(jnp.int32, (tokens, tokens), 0)
    lane = lax.broadcasted_iota(jnp.int32, (tokens, tokens), 1)
    row = jnp.sum(jnp.where(at == lane, square, 0.0), axis=0, keepdims=True)
    out[...] = jnp.broadcast_to(row[None], out.shape)


def norm_kernel(squares, rows, gain, out):
    wide = rows[...].astype(jnp.float32)
    tokens = wide.shape[0]
    row = jnp.sum(squares[...], axis=0)
    at = lax.broadcasted_iota(jnp.int32, (tokens, tokens), 0)
    lane = lax.broadcasted_iota(jnp.int32, (tokens, tokens), 1)
    square = jnp.sum(jnp.where(at == lane, row, 0.0), axis=1, keepdims=True)
    out[...] = (wide * lax.rsqrt(square / D + EPS) * gain[...]).astype(jnp.bfloat16)


def small_call(kernel, shape, dtype, *operands):
    return pl.pallas_call(
        kernel,
        out_shape=jax.ShapeDtypeStruct(shape, dtype),
        in_specs=[pl.BlockSpec(memory_space=pltpu.VMEM)] * len(operands),
        out_specs=pl.BlockSpec(memory_space=pltpu.VMEM),
        compiler_params=pltpu.CompilerParams(vmem_limit_bytes=8 * 1024 * 1024),
    )(*operands)


def key_row(position):
    step, at = divmod(position, PIECE)
    return step * (PIECE + VALUE_ROWS * (PIECE // LANES)) + at


def value_row(position):
    step, at = divmod(position, PIECE)
    return key_row(step * PIECE) + PIECE + at // LANES * VALUE_ROWS


def prepare_kernel(length, keys, values, out):
    count = keys.shape[0]
    valid = length[0]
    at = lax.broadcasted_iota(jnp.int32, (HD, HD), 0)
    lane = lax.broadcasted_iota(jnp.int32, (HD, HD), 1)
    unit = jnp.where(at == lane, 1.0, 0.0).astype(jnp.bfloat16)

    def write(masked):
        for start in range(0, count, PIECE):
            own_keys = keys[start : start + PIECE, :]
            own_values = values[start : start + PIECE, :]
            if masked:
                inside = start + lax.broadcasted_iota(jnp.int32, (PIECE, HD), 0) < valid
                first = keys[0:16, :].astype(jnp.float32)[0:1, :]
                own_keys = jnp.where(inside, own_keys.astype(jnp.float32), first)
                own_keys = own_keys.astype(jnp.bfloat16)
                own_values = jnp.where(inside, own_values.astype(jnp.float32), 0.0)
                own_values = own_values.astype(jnp.bfloat16)
            out[key_row(start) : key_row(start) + PIECE, :] = own_keys
            across = lax.dot_general(
                unit, own_values, (((1,), (1,)), ((), ())), preferred_element_type=jnp.float32
            ).astype(jnp.bfloat16)
            for block in range(0, PIECE, LANES):
                row = value_row(start + block)
                out[row : row + HD, :] = across[:, block : block + LANES]
                ones = jnp.ones((ONES_ROWS, LANES), jnp.float32)
                if masked:
                    place = lax.broadcasted_iota(jnp.int32, (ONES_ROWS, LANES), 1)
                    ones = jnp.where(start + block + place < valid, ones, 0.0)
                out[row + HD : row + VALUE_ROWS, :] = ones.astype(jnp.bfloat16)

    pl.when(valid >= count)(functools.partial(write, False))
    pl.when(valid < count)(functools.partial(write, True))


def prepare(lengths, keys, values):
    count = keys.shape[0]
    return pl.pallas_call(
        prepare_kernel,
        out_shape=jax.ShapeDtypeStruct((key_row(count), HD), jnp.bfloat16),
        in_specs=[
            pl.BlockSpec(memory_space=pltpu.SMEM),
            pl.BlockSpec(memory_space=pltpu.VMEM),
            pl.BlockSpec(memory_space=pltpu.VMEM),
        ],
        out_specs=pl.BlockSpec(memory_space=pltpu.VMEM),
        compiler_params=pltpu.CompilerParams(vmem_limit_bytes=16 * 1024 * 1024),
        cost_estimate=pl.CostEstimate(
            flops=8 * count * HD, bytes_accessed=8 * count * HD, transcendentals=0
        ),
    )(lengths, keys, values)


def attend_kernel(query, here, there, out, scores, *, chunks, count):
    tokens = query.shape[0]
    wide = 2 * tokens
    cache = (here, there)
    reach = scores.shape[1]
    pairs = OWN // 2
    unit = math.log2(math.e) / math.sqrt(HD)
    units = [
        (half, start, pair)
        for half in range(CORES)
        for start in range(0, count, reach)
        for pair in range(pairs)
    ]

    def query_pair(pair):
        base = pair * 2 * HD
        return jnp.concatenate(
            [query[:, base : base + HD], query[:, base + HD : base + 2 * HD]], axis=0
        )

    queries = [query_pair(pair) for pair in range(pairs)]

    def score_piece(number, offset, top):
        half, start, pair = units[number]
        row = key_row(start + offset)
        part = lax.dot_general(
            cache[half][row : row + STEP, :],
            queries[pair],
            (((1,), (1,)), ((), ())),
            preferred_element_type=jnp.float32,
        )
        scores[number % 2, offset : offset + STEP, :] = part
        return jnp.maximum(top, jnp.max(part.reshape(STEP // 8, 8, wide), axis=0))

    lowest = jnp.full((8, wide), -jnp.inf, jnp.float32)
    top = lowest
    for offset in range(0, reach, STEP):
        top = score_piece(0, offset, top)
    held = [[] for _ in range(pairs)]
    for number, (half, start, pair) in enumerate(units):
        best = jnp.max(top, axis=0, keepdims=True)
        top = lowest
        accum = None
        for offset in range(0, reach, PIECE):
            if number + 1 < len(units):
                top = score_piece(number + 1, offset, top)
            weight = jnp.exp2((scores[number % 2, offset : offset + PIECE, :] - best) * unit)
            across = [
                cache[half][value_row(at) : value_row(at) + VALUE_ROWS, :]
                for at in range(start + offset, start + offset + PIECE, LANES)
            ]
            product = jnp.dot(
                jnp.concatenate(across, axis=1),
                weight.astype(jnp.bfloat16),
                preferred_element_type=jnp.float32,
            )
            accum = product if accum is None else accum + product
            if number + 1 < len(units):
                top = score_piece(number + 1, offset + STEP, top)
        held[pair].append((best, accum))

    for pair in range(pairs):
        best = functools.reduce(jnp.maximum, [own for own, _ in held[pair]])
        accum = sum(part * jnp.exp2((own - best) * unit) for own, part in held[pair])
        total = accum[HD : HD + 1, :]
        level = best * unit + jnp.log2(total)
        high = jnp.where(jnp.abs(level) < 1.0, 0.0, level).astype(jnp.bfloat16).astype(jnp.float32)
        rest = level - high
        middle = rest.astype(jnp.bfloat16).astype(jnp.float32)
        stats = jnp.concatenate(
            [
                high * (1.0 / LEVEL_STEP),
                middle,
                (rest - middle) * LEVEL_STEP,
                jnp.zeros((STAT_ROWS - 3, wide), jnp.float32),
            ],
            axis=0,
        )
        mean = accum[0:HD, :] * (ACCUM_SCALE / total)
        per_head = chunks // OWN
        rows = HD // per_head
        for side in range(2):
            lanes = slice(side * tokens, (side + 1) * tokens)
            for part in range(per_head):
                chunk = (2 * pair + side) * per_head + part
                out[chunk, 0:rows, :] = mean[part * rows : (part + 1) * rows, lanes]
                out[chunk, rows : rows + STAT_ROWS, :] = stats[:, lanes]


def attend(query, here, there, count, chunks):
    tokens = query.shape[0]
    rows = OWN * HD // chunks
    return pl.pallas_call(
        functools.partial(attend_kernel, chunks=chunks, count=count),
        out_shape=jax.ShapeDtypeStruct((chunks, rows + STAT_ROWS, tokens), jnp.float32),
        in_specs=[pl.BlockSpec(memory_space=pltpu.VMEM)] * 3,
        out_specs=pl.BlockSpec(memory_space=pltpu.VMEM),
        scratch_shapes=[pltpu.VMEM((2, min(count, REACH), 2 * tokens), jnp.float32)],
        compiler_params=pltpu.CompilerParams(vmem_limit_bytes=24 * 1024 * 1024),
        cost_estimate=pl.CostEstimate(
            flops=4 * GROUP * tokens * count * HD,
            bytes_accessed=8 * count * HD,
            transcendentals=GROUP * tokens * count,
        ),
    )(query, here, there)


def local(span, gain, w_query, keys, values, lengths, w_out):
    chips = lax.axis_size("z")
    shards = CORES * chips
    heads = lax.axis_size("tp")
    own = span[0]
    step = own.shape[0]
    tokens = heads * step
    width = GROUP * HD

    here = prepare(lengths, keys[0, :, 0, :], values[0, :, 0, :])
    span_rows = spread(own, "tp").reshape(tokens, -1)
    span_rows, here = lax.optimization_barrier((span_rows, here))
    there = from_behind(here, "core", 1)

    squares = small_call(square_kernel, (shards, 1, tokens), jnp.float32, span_rows)
    squares = lax.all_to_all(squares, ("core", "z"), 0, 0)
    normed = small_call(norm_kernel, span_rows.shape, jnp.bfloat16, squares, span_rows, gain)
    partial = jnp.dot(normed, w_query[0], preferred_element_type=jnp.float32) * QUERY_SCALE
    partial = partial.astype(jnp.float16).reshape(tokens, CORES, width // CORES)
    partial = jnp.swapaxes(partial, 0, 1).reshape(shards, tokens // chips, width // CORES)
    parts = lax.all_to_all(partial, ("core", "z"), 0, 0)
    query = jnp.sum(parts.astype(jnp.float32), axis=0) * (1.0 / QUERY_SCALE)
    query = spread(query.astype(jnp.bfloat16), "z").reshape(tokens, width // CORES)

    rows = width // shards
    pieces = attend(query, here, there, keys.shape[1], chips).astype(jnp.float16)
    pieces = lax.all_to_all(pieces, "z", 0, 0).astype(jnp.float32)
    level = (
        pieces[:, rows, :] * LEVEL_STEP
        + pieces[:, rows + 1, :]
        + pieces[:, rows + 2, :] * (1.0 / LEVEL_STEP)
    )
    factor = jnp.exp2(level - jnp.max(level, axis=0, keepdims=True))
    numer = jnp.sum(pieces[:, :rows, :] * factor[:, None, :], axis=0)
    denom = jnp.sum(factor, axis=0, keepdims=True) * ACCUM_SCALE
    attended = spread((numer / denom).astype(jnp.bfloat16), ("core", "z")).reshape(width, tokens)

    projected = lax.dot_general(
        attended, w_out[0], (((0,), (0,)), ((), ())), preferred_element_type=jnp.float32
    )
    projected = (projected * OUT_SCALE).astype(jnp.float16).reshape(heads, step, -1)
    parts = lax.all_to_all(projected, "tp", 0, 0).astype(jnp.float32)
    updated = (own.astype(jnp.float32) + jnp.sum(parts, axis=0) * (1.0 / OUT_SCALE)).astype(jnp.bfloat16)
    return from_behind(updated, "section", 1)[None]


def solution(mesh):
    shards, sections, heads = (mesh.shape[name] for name in ("kvp", "section", "tp"))
    split = Mesh(
        mesh.devices.reshape(shards // CORES, CORES, sections, heads),
        ("z", "core", "section", "tp"),
    )
    shard = ("z", "core")
    in_specs = (
        P("section", "tp", shard),
        P("section", shard),
        P("section", shard, "tp"),
        P("section", shard, "tp", None),
        P("section", shard, "tp", None),
        P(shard),
        P("section", "tp", shard),
    )
    out_specs = P("section", "tp", shard)
    return jax.shard_map(local, mesh=split, in_specs=in_specs, out_specs=out_specs, check_vma=False)
```
